256 devices in a mesh: tile: 64 (over x, z, core), depth: 4 (over y).
Axes of the slice: x: 4, y: 4, z: 8, core: 2. Of those that a mesh axis runs over, the one named last changes fastest.
Arguments:
- reference_image: float32 [32, 2048, 128], P('depth', 'tile'), may hold values from -120 to 120, as said below
- deformed_image: float32 [32, 2048, 128], P('depth', 'tile'), may hold values from -120 to 120, as said below
- offsets: int32 [3, 32, 2048, 128], P(None, 'depth', 'tile'), may hold values from -2 to 1, as said below
- node_ids: int32 [2, 128, 8], P(None, 'tile'), may hold values from 0 to 2047, as said below
- start_motion: float32 [3, 2048], P(None, 'tile'), may hold values from -0.6 to 0.6
Outputs:
- displacement: float32 [3, 2048], P(None, 'tile')
- misfit: float32 [3], replicated
- residual_field: float32 [32, 2048, 128], P('depth', 'tile')
The draws below stay inside these ranges and needn't reach their ends.
Inputs may be any that keep to these rules, and one draw needn't show every extreme that they name: `node_ids`: every number from 0 to 2047 stands once; the nodes at first in-plane layers k with k // 2 = t carry the numbers t * 32 to (t + 1) * 32 - 1. `offsets`: each component is constant over each element, the blocks of 16 x 16 x 16 voxels between node layers. `reference_image`: gray values. `deformed_image`: gray values.
All inputs are finite; a program needn't handle non-finite values.
Results may differ from the reference program's by a relative error of at most 0.0055.
Values sent between devices are 32-bit elements; how exact they have to be, the bound alone decides.
No kernel may reach another device: no remote copies, remote signals or barrier semaphores. Data moves between devices by JAX's collectives and lax.ppermute only.
A program may use at most 64 MiB of HBM per device.

```python
import math
import jax
import jax.numpy as jnp
from jax import lax

ELEM = 16
SLAB = 32
CX = 32
YCELLS = 128
ITERS = 3
XCELLS = 2048
EXD = 2
EZ = 2
EY = 8
EX = 128
NODES = 2048


def element_offsets(key):
    table = jax.random.randint(jax.random.fold_in(key, 51), (3, EZ, EX, EY), -2, 2, jnp.int32)
    table = jnp.repeat(table, ELEM, axis=1)
    table = jnp.repeat(table, ELEM, axis=2)
    return jnp.repeat(table, ELEM, axis=3).astype(jnp.int32)


def voxel_grid():
    shape_full = (SLAB, XCELLS, YCELLS)
    z_grid = jnp.broadcast_to(jnp.arange(SLAB, dtype=jnp.int32)[:, None, None], shape_full)
    x_grid = jnp.broadcast_to(jnp.arange(XCELLS, dtype=jnp.int32)[None, :, None], shape_full)
    y_grid = jnp.broadcast_to(jnp.arange(YCELLS, dtype=jnp.int32)[None, None, :], shape_full)
    return jnp.stack([z_grid, x_grid, y_grid])


def true_motion(key, grid, spread):
    rates = jax.random.randint(jax.random.fold_in(key, 14), (3, 3), 1, 3, jnp.int32)
    means = jax.random.uniform(jax.random.fold_in(key, 15), (3,), jnp.float32, 0.25, 0.4)
    angles = jax.random.uniform(jax.random.fold_in(key, 16), (3,), jnp.float32, -math.pi, math.pi)
    width = 4 * ELEM
    pieces = []
    for comp in range(3):
        whole = jnp.mod(rates[comp, 0] * grid[0] + rates[comp, 1] * grid[1] + rates[comp, 2] * grid[2], width)
        pieces.append(means[comp] + spread * jnp.sin(2.0 * math.pi / width * whole.astype(jnp.float32) + angles[comp]))
    return jnp.stack(pieces)


def texture(key, lattice, fraction):
    wave_count = 16
    period = 64
    waves = jax.random.randint(jax.random.fold_in(key, 12), (wave_count, 3), -6, 7, jnp.int32)
    phases = jax.random.uniform(jax.random.fold_in(key, 13), (wave_count,), jnp.float32, -math.pi, math.pi)
    total = jnp.zeros(lattice.shape[1:], jnp.float32)
    for index in range(wave_count):
        whole = jnp.mod(waves[index, 0] * lattice[0] + waves[index, 1] * lattice[1] + waves[index, 2] * lattice[2], period)
        part = waves[index, 0].astype(jnp.float32) * fraction[0] + waves[index, 1].astype(jnp.float32) * fraction[1] + waves[index, 2].astype(jnp.float32) * fraction[2]
        total = total + jnp.cos(2.0 * math.pi / period * (whole.astype(jnp.float32) + part) + phases[index])
    return total / wave_count


def smooth_scale(lattice, fraction, rise_x, rise_y):
    place_x = jnp.clip((lattice[1].astype(jnp.float32) + fraction[1]) / (XCELLS - 1), 0.0, 1.0)
    place_y = jnp.clip((lattice[2].astype(jnp.float32) + fraction[2]) / (YCELLS - 1), 0.0, 1.0)
    return jnp.exp(math.log(rise_x) * place_x + math.log(rise_y) * place_y)


def image_pair(key, image_index):
    shape_full = (SLAB, XCELLS, YCELLS)
    grid = voxel_grid()
    spread = 0.12
    if image_index == 0:
        lattice = grid + element_offsets(key)
        fraction = true_motion(key, grid, spread)
    else:
        lattice = grid
        fraction = jnp.zeros((3,) + shape_full, jnp.float32)
    pattern_base = texture(key, lattice, fraction)
    noise_key = jax.random.fold_in(key, 30 + image_index)
    scale = smooth_scale(lattice, fraction, 3.0, 10.0)
    noise = 0.033 * jax.random.truncated_normal(noise_key, -3.0, 3.0, shape_full, jnp.float32)
    pattern = 3.85 * pattern_base
    return (scale * (pattern + noise)).astype(jnp.float32)


def draw_reference_image(key, part):
    return image_pair(key, 0)


def draw_deformed_image(key, part):
    return image_pair(key, 1)


def draw_offsets(key, part):
    return element_offsets(key)


def draw_node_ids(key, part):
    key = jax.random.fold_in(key, 41)
    tile_total = XCELLS // CX
    per_tile = EZ * EXD * EY
    tile_keys = jax.random.split(key, tile_total)

    def shuffle(item_key):
        return jax.random.permutation(item_key, per_tile)
    orders = jax.vmap(shuffle)(tile_keys).astype(jnp.int32)
    numbers = orders + (jnp.arange(tile_total, dtype=jnp.int32) * per_tile)[:, None]
    blocks = numbers.reshape(tile_total, EZ, EXD, EY).transpose(1, 0, 2, 3)
    return blocks.reshape(EZ, tile_total * EXD, EY).astype(jnp.int32)


def shard_levels(key, extent, cuts, low, largest):
    def one(position, blocks):
        heights = jax.random.uniform(jax.random.fold_in(jax.random.fold_in(key, 6), position), (blocks,), jnp.float32, low / len(cuts), largest / len(cuts))
        return jnp.repeat(jnp.exp(heights), extent[position] // blocks).reshape((-1,) + (1,) * (len(extent) - position - 1))

    level = one(*cuts[0])
    for cut in cuts[1:]:
        level = level * one(*cut)
    return level


def bell_draw(stream_key, dims, deviation, limit, cuts=(), kind=jnp.bfloat16):
    entries = deviation * jax.random.normal(stream_key, dims, jnp.float32)
    if cuts:
        entries = entries * shard_levels(stream_key, dims, cuts, -0.22, 0.18)
    return jnp.clip(entries, -limit, limit).astype(kind)


def setup_inputs(seed: int = 0) -> dict:
    keys = jax.random.split(jax.random.key(seed), 6)
    return {
        "reference_image": draw_reference_image(jax.random.fold_in(keys[5], 71), 0),
        "deformed_image": draw_deformed_image(jax.random.fold_in(keys[5], 71), 0),
        "offsets": draw_offsets(jax.random.fold_in(keys[5], 71), 0),
        "node_ids": draw_node_ids(jax.random.fold_in(keys[5], 71), 0),
        "start_motion": bell_draw(keys[4], (3, NODES), 0.15, 0.6, ((1, 64),), jnp.float32),
    }


highest = lax.Precision.HIGHEST


def hat_matrix(voxel_start, voxel_count, node_start, node_count):
    centers = (jnp.arange(voxel_count, dtype=jnp.int32) + voxel_start).astype(jnp.float32) + 0.5
    places = ((jnp.arange(node_count, dtype=jnp.int32) + node_start) * ELEM).astype(jnp.float32)
    return jnp.maximum(1.0 - jnp.abs(centers[:, None] - places[None, :]) / ELEM, 0.0)


def interpolate(node_values, weight_z, weight_x, weight_y):
    along_x = jnp.einsum("cakb,xk->caxb", node_values, weight_x, precision=highest)
    along_y = jnp.einsum("caxb,yb->caxy", along_x, weight_y, precision=highest)
    return jnp.einsum("caxy,za->czxy", along_y, weight_z, precision=highest)


def restrict(voxel_field, weight_z, weight_x, weight_y):
    over_z = jnp.einsum("czxy,za->caxy", voxel_field, weight_z, precision=highest)
    over_y = jnp.einsum("caxy,yb->caxb", over_z, weight_y, precision=highest)
    return jnp.einsum("caxb,xk->cakb", over_y, weight_x, precision=highest)


def corner_weight(motion, corner):
    factor_z = motion[0] if corner // 4 % 2 else 1.0 - motion[0]
    factor_x = motion[1] if corner // 2 % 2 else 1.0 - motion[1]
    factor_y = motion[2] if corner % 2 else 1.0 - motion[2]
    return factor_z * factor_x * factor_y


def corner_shift(corner, stride_z, stride_x):
    return (corner // 4 % 2) * stride_z + (corner // 2 % 2) * stride_x + corner % 2


def gradient(padded):
    slope_z = (padded[:-4, 2:-2, 2:-2] - padded[4:, 2:-2, 2:-2] + 8.0 * (padded[3:-1, 2:-2, 2:-2] - padded[1:-3, 2:-2, 2:-2])) / 12.0
    slope_x = (padded[2:-2, :-4, 2:-2] - padded[2:-2, 4:, 2:-2] + 8.0 * (padded[2:-2, 3:-1, 2:-2] - padded[2:-2, 1:-3, 2:-2])) / 12.0
    slope_y = (padded[2:-2, 2:-2, :-4] - padded[2:-2, 2:-2, 4:] + 8.0 * (padded[2:-2, 2:-2, 3:-1] - padded[2:-2, 2:-2, 1:-3])) / 12.0
    return jnp.stack([slope_z, slope_x, slope_y])


def reference(reference_image, deformed_image, offsets, node_ids, start_motion):
    levenberg = 0.1 * ELEM ** 3
    weight_z = hat_matrix(0, SLAB, 0, EZ)
    weight_x = hat_matrix(0, XCELLS, 0, EX)
    weight_y = hat_matrix(0, YCELLS, 0, EY)
    flat_image = jnp.pad(deformed_image, 2).reshape(-1)
    stride_x = YCELLS + 4
    stride_z = (XCELLS + 4) * stride_x
    z_coord = jnp.arange(SLAB, dtype=jnp.int32)[:, None, None]
    x_coord = jnp.arange(XCELLS, dtype=jnp.int32)[None, :, None]
    y_coord = jnp.arange(YCELLS, dtype=jnp.int32)[None, None, :]
    base_index = ((z_coord + 2 + offsets[0]) * stride_z + (x_coord + 2 + offsets[1]) * stride_x + (y_coord + 2 + offsets[2])).astype(jnp.int32)
    node_motion = start_motion[:, node_ids]
    full_count = float(SLAB * XCELLS * YCELLS)
    misfits = []
    residual = jnp.zeros((SLAB, XCELLS, YCELLS), jnp.float32)
    for iteration in range(ITERS):
        motion = interpolate(node_motion, weight_z, weight_x, weight_y)
        warped = jnp.zeros((SLAB, XCELLS, YCELLS), jnp.float32)
        for corner in range(8):
            picked = jnp.take(flat_image, base_index + corner_shift(corner, stride_z, stride_x))
            warped = warped + corner_weight(motion, corner) * picked
        residual = warped - reference_image
        misfits.append(jnp.sum(residual * residual) / full_count)
        slopes = gradient(jnp.pad(warped, 2))
        node_force = restrict(slopes * residual[None], weight_z, weight_x, weight_y)
        node_stiffness = restrict(slopes * slopes, weight_z * weight_z, weight_x * weight_x, weight_y * weight_y)
        direction = node_force / (node_stiffness + levenberg)
        descent = jnp.sum(node_force * direction)
        length = jnp.sum(direction * direction)
        projected = jnp.sum(slopes * interpolate(direction, weight_z, weight_x, weight_y), axis=0)
        curvature = jnp.sum(projected * projected) + levenberg * length
        node_motion = node_motion - (descent / curvature) * direction
    displacement = jnp.zeros((3, NODES), jnp.float32).at[:, node_ids.reshape(-1)].set(node_motion.reshape(3, -1))
    return displacement, jnp.stack(misfits), residual
```

```python
import functools

import jax
import jax.numpy as jnp
import numpy as np
from jax import lax
from jax.experimental import pallas as pl
from jax.experimental.pallas import tpu as pltpu
from jax.sharding import PartitionSpec as P

ELEM = 16
ITERS = 3
SLAB = 32
ROWS = 32
LANES = 128
HALO = 24
FRAME = ROWS + 2 * HALO
GROUPS = FRAME // 8
LEVENBERG = 0.1 * ELEM**3
VOXELS = 8388608.0
F32 = jnp.float32

highest = lax.Precision.HIGHEST


def hat(centers, places):
    return np.maximum(1.0 - np.abs(centers[:, None] - places[None, :]) / ELEM, 0.0)


def constants():
    frame = np.arange(FRAME) - HALO + 0.5
    along_x = np.zeros((6, FRAME, 4, 16), np.float32)
    for tile in range(4):
        for k in range(2):
            column = hat(frame, np.array([(2 * (tile - 1) + k) * ELEM]))[:, 0]
            for ca in range(6):
                along_x[ca, :, tile, k * 6 + ca] = column
    along_y = hat(np.arange(LANES) + 0.5, (np.arange(LANES) % 8) * ELEM).astype(np.float32)
    return (
        along_x.reshape(6 * FRAME, 64),
        np.ascontiguousarray(along_y.T),
        along_y,
        along_y * along_y,
    )


def dot(left, right):
    return jnp.dot(left, right, precision=highest, preferred_element_type=F32)


def lane_ids(shape):
    return lax.broadcasted_iota(jnp.int32, shape, 1)


def row_ids(shape):
    return lax.broadcasted_iota(jnp.int32, shape, 0)


def pack_body(with_extra, halo, place, own, one, two, three, *refs):
    if with_extra:
        extra, full, low, high = refs
    else:
        full, low, high = refs
    depth = place[1]
    for step, piece in enumerate((own, one, two, three)):
        start = lax.rem(depth + step, 4) * 8
        block = piece[...]
        full[pl.ds(start, 8)] = block
        low[pl.ds(start, 8)] = block[:, :halo]
        high[pl.ds(start, 8)] = block[:, ROWS - halo :]
    if with_extra:
        low[SLAB] = extra[...]
        high[SLAB] = extra[...]


def pack(place, pieces, halo, extra=None):
    planes = SLAB + (extra is not None)
    shapes = [
        jax.ShapeDtypeStruct((SLAB, ROWS, LANES), F32),
        jax.ShapeDtypeStruct((planes, halo, LANES), F32),
        jax.ShapeDtypeStruct((planes, halo, LANES), F32),
    ]
    vmem = pl.BlockSpec(memory_space=pltpu.VMEM)
    args = [place, *pieces] + ([extra] if extra is not None else [])
    return pl.pallas_call(
        functools.partial(pack_body, extra is not None, halo),
        out_shape=shapes,
        in_specs=[pl.BlockSpec(memory_space=pltpu.SMEM)] + [vmem] * (len(args) - 1),
        out_specs=[vmem] * 3,
        cost_estimate=pl.CostEstimate(flops=0, bytes_accessed=2000000, transcendentals=0),
        name="pack",
    )(*args)


def corner_body(tiles, place, full, left, right, extra, cor, source, shifted, table, chunk, sems):
    tile = place[0]
    zero = jnp.zeros((2, FRAME + 16, LANES), F32)
    source[0:2] = zero
    source[SLAB + 2 : SLAB + 4] = zero
    edge = jnp.zeros((SLAB, 8, LANES), F32)
    source[2 : SLAB + 2, 0:8] = edge
    source[2 : SLAB + 2, 8 + FRAME : 16 + FRAME] = edge
    source[2 : SLAB + 2, 8 : 8 + HALO] = left[0:SLAB]
    source[2 : SLAB + 2, 8 + HALO : 8 + HALO + ROWS] = full[...]
    source[2 : SLAB + 2, 8 + HALO + ROWS : 8 + FRAME] = right[0:SLAB]
    sides = ((left, 0), (left, 1), (extra, 0), (extra, 1), (right, 0), (right, 1))
    for ex, (side, which) in enumerate(sides):
        for e in range(2):
            for c in range(3):
                at = e * 6 + c * 2 + which
                row = side[at : at + 1] if side is extra else side[SLAB, at : at + 1]
                place_at = (e * 6 + ex) * 3 + c
                table[place_at : place_at + 1] = row

    shape = (8, LANES)
    lanes = lane_ids(shape)

    def group(v, carry):
        ex = (v + 1) // 2
        outside = ((tile == 0) & (v < 3)) | ((tile == tiles - 1) & (v >= 7))
        inside = jnp.where(outside, 0.0, 1.0).astype(F32)
        for e in range(2):
            offs = [
                jnp.broadcast_to(table[pl.ds((e * 6 + ex) * 3 + c, 1)], shape) for c in range(3)
            ]
            base = lanes + offs[2].astype(jnp.int32)
            picks = []
            for s in range(2):
                at = base + s
                good = jnp.where((at >= 0) & (at < LANES), inside, 0.0)
                picks.append((jnp.clip(at, 0, LANES - 1), good))
            for p in range(20):
                for half in range(2):
                    block = source[16 * e + p, pl.ds(8 * v + 6 + 4 * half, 8)]
                    for s in range(2):
                        index, good = picks[s]
                        taken = jnp.take_along_axis(block, index, axis=1, mode="promise_in_bounds")
                        shifted[s, p, 4 * half : 4 * half + 8] = taken * good
            is_x = [offs[1] == float(o) for o in (-2, -1, 0)]
            is_z = [offs[0] == float(o) for o in (-2, -1, 0)]
            window = []
            for p in range(20):
                corners = []
                for sx in range(2):
                    for sy in range(2):
                        rows = [shifted[sy, p, sx + o : sx + o + 8] for o in range(4)]
                        corners.append(
                            jnp.where(
                                is_x[0],
                                rows[0],
                                jnp.where(is_x[1], rows[1], jnp.where(is_x[2], rows[2], rows[3])),
                            )
                        )
                window.append(corners)
                if p >= 3:
                    c00, c01, c10, c11 = [
                        jnp.where(
                            is_z[0],
                            window[p - 3][n],
                            jnp.where(
                                is_z[1],
                                window[p - 2][n],
                                jnp.where(is_z[2], window[p - 1][n], window[p][n]),
                            ),
                        )
                        for n in range(4)
                    ]
                    chunk[v, e, p - 3, 0] = c00
                    chunk[v, e, p - 3, 1] = c01 - c00
                    chunk[v, e, p - 3, 2] = c10 - c00
                    chunk[v, e, p - 3, 3] = (c11 - c10) - (c01 - c00)
        pltpu.make_async_copy(chunk.at[v], cor.at[v], sems.at[v]).start()
        return carry

    lax.fori_loop(0, GROUPS, group, 0)
    for v in range(GROUPS):
        pltpu.make_async_copy(chunk.at[v], cor.at[v], sems.at[v]).wait()


def corner_images(tiles, place, full, left, right, extra):
    vmem = pl.BlockSpec(memory_space=pltpu.VMEM)
    shape = (GROUPS, 2, 17, 4, 8, LANES)
    return pl.pallas_call(
        functools.partial(corner_body, tiles),
        out_shape=jax.ShapeDtypeStruct(shape, F32),
        in_specs=[pl.BlockSpec(memory_space=pltpu.SMEM)] + [vmem] * 4,
        out_specs=pl.BlockSpec(memory_space=pl.ANY),
        scratch_shapes=[
            pltpu.VMEM((SLAB + 4, FRAME + 16, LANES), F32),
            pltpu.VMEM((2, 20, 16, LANES), F32),
            pltpu.VMEM((40, LANES), F32),
            pltpu.VMEM(shape, F32),
            pltpu.SemaphoreType.DMA((GROUPS,)),
        ],
        cost_estimate=pl.CostEstimate(flops=10000000, bytes_accessed=9000000, transcendentals=0),
        name="corners",
        compiler_params=pltpu.CompilerParams(vmem_limit_bytes=48 * 2**20),
    )(place, full, left, right, extra)


def updated_motion(motion, received, tile, tiles, padded):
    padded[...] = jnp.zeros_like(padded)
    padded[8 : 8 + tiles] = received[...]
    total = jnp.sum(received[...], axis=0, keepdims=True)
    descent = total[:, 96:97]
    length = total[:, 97:98]
    curvature = total[:, 98:99]
    step = descent / (curvature + LEVENBERG * length)
    near = padded[pl.ds(7 + tile, 8)]
    return motion[...] - step * near


def iteration_body(tiles, first, last, place, *refs):
    refs = list(refs)
    motion = refs.pop(0)
    received = None if first else refs.pop(0)
    ref_left, ref_own, ref_right, cor, along_x, along_y, over_y, over_y2 = refs[:8]
    refs = refs[8:]
    block_out, motion_out = refs[:2]
    refs = refs[2:]
    residual_out = refs.pop(0) if last else None
    cors, wide, warped, slopes, layers, rows_f, rows_s, padded = refs[:8]
    refs = refs[8:]
    residuals = refs.pop(0) if last else None
    sems = refs.pop(0)

    for v in range(GROUPS):
        pltpu.make_async_copy(cor.at[v], cors.at[v], sems.at[v]).start()

    tile = place[0]
    low_flag = jnp.where(tile > 0, 1.0, 0.0).astype(F32)
    high_flag = jnp.where(tile < tiles - 1, 1.0, 0.0).astype(F32)
    now = motion[...] if first else updated_motion(motion, received, tile, tiles, padded)
    motion_out[...] = now
    shape16 = (16, LANES)
    pick = (lane_ids(shape16) // 8 == row_ids(shape16)) & (row_ids(shape16) < 12)
    spread = jnp.concatenate(
        [jnp.where(pick, jnp.broadcast_to(now[n : n + 1], shape16), 0.0) for n in range(4)], axis=0
    )
    wide[...] = dot(along_x[...], dot(spread, along_y[...]))

    zero = jnp.zeros((2, FRAME, LANES), F32)
    warped[0:2] = zero
    warped[SLAB + 2 : SLAB + 4] = zero

    def warp(v, carry):
        pltpu.make_async_copy(cor.at[v], cors.at[v], sems.at[v]).wait()
        at = pl.ds(pl.multiple_of(8 * v, 8), 8)
        near = [wide[pl.ds(pl.multiple_of(2 * c * FRAME + 8 * v, 8), 8)] for c in range(3)]
        far = [wide[pl.ds(pl.multiple_of((2 * c + 1) * FRAME + 8 * v, 8), 8)] for c in range(3)]
        for e in range(2):
            if e == 0:
                move = [n + (f - n) * (1.0 / 32) for n, f in zip(near, far)]
                gain = [(f - n) * (1.0 / 16) for n, f in zip(near, far)]
            else:
                move = [f * (31.0 / 32) for f in far]
                gain = [f * (-1.0 / 16) for f in far]
            plane = [cors[v, e, 0, n] for n in range(4)]
            for j in range(16):
                above = [cors[v, e, j + 1, n] for n in range(4)]
                mz, mx, my = move
                here = (plane[0] + my * plane[1]) + mx * (plane[2] + my * plane[3])
                there = (above[0] + my * above[1]) + mx * (above[2] + my * above[3])
                warped[2 + 16 * e + j, at] = here + mz * (there - here)
                plane = above
                if j < 15:
                    move = [m + g for m, g in zip(move, gain)]
        return carry

    lax.fori_loop(0, GROUPS, warp, 0)

    shape = (8, LANES)
    lanes = lane_ids(shape)
    ahead_1 = jnp.where(lanes < LANES - 1, 8.0, 0.0)
    behind_1 = jnp.where(lanes > 0, 8.0, 0.0)
    ahead_2 = jnp.where(lanes < LANES - 2, 1.0, 0.0)
    behind_2 = jnp.where(lanes > 1, 1.0, 0.0)
    zeros = jnp.zeros(shape, F32)

    def slope_group(v, target, target_start, own, misfit):
        at = pl.ds(pl.multiple_of(8 * v, 8), 8)
        row = pl.multiple_of(8 * (v - target_start), 8)
        planes = [warped[n, at] for n in range(4)]
        for e in range(2):
            first_sum = [zeros] * 3
            second_sum = [zeros] * 3
            squares_0 = [zeros] * 3
            squares_1 = [zeros] * 3
            for j in range(16):
                z = 16 * e + j
                planes.append(warped[z + 4, at])
                mid = planes[2]
                slope_z = 8.0 * (planes[3] - planes[1]) - (planes[4] - planes[0])
                planes = planes[1:]
                up_1 = warped[z + 2, pl.ds(8 * v + 1, 8)]
                up_2 = warped[z + 2, pl.ds(8 * v + 2, 8)]
                down_1 = warped[z + 2, pl.ds(8 * v - 1, 8)]
                down_2 = warped[z + 2, pl.ds(8 * v - 2, 8)]
                slope_x = 8.0 * (up_1 - down_1) - (up_2 - down_2)
                slope_y = (
                    ahead_1 * pltpu.roll(mid, LANES - 1, 1) - behind_1 * pltpu.roll(mid, 1, 1)
                ) - (ahead_2 * pltpu.roll(mid, LANES - 2, 1) - behind_2 * pltpu.roll(mid, 2, 1))
                residual = mid - target[z, pl.ds(row, 8)]
                three = (slope_z, slope_x, slope_y)
                if own:
                    misfit = misfit + residual * residual
                    for c in range(3):
                        slopes[c, z, pl.ds(row, 8)] = three[c]
                    if last:
                        residuals[z, pl.ds(row, 8)] = residual
                weight = 1.0 - (j + 0.5) / 16.0
                for c in range(3):
                    first_sum[c] = first_sum[c] + three[c] * residual
                    second_sum[c] = second_sum[c] + first_sum[c]
                    square = three[c] * three[c]
                    squares_0[c] = squares_0[c] + (weight * weight) * square
                    if e == 0:
                        squares_1[c] = squares_1[c] + ((1.0 - weight) ** 2) * square
            for c in range(3):
                falling = (second_sum[c] - 0.5 * first_sum[c]) * (1.0 / 16)
                if e == 0:
                    layers[v - 1, 2 * c] = falling
                    layers[v - 1, 2 * c + 1] = first_sum[c] - falling
                    layers[v - 1, 6 + 2 * c] = squares_0[c]
                    layers[v - 1, 6 + 2 * c + 1] = squares_1[c]
                else:
                    layers[v - 1, 2 * c + 1] += falling
                    layers[v - 1, 6 + 2 * c + 1] += squares_0[c]
        return misfit

    lax.fori_loop(1, 3, lambda v, m: slope_group(v, ref_left, 1, False, m), zeros)
    misfit = lax.fori_loop(3, 7, lambda v, m: slope_group(v, ref_own, 3, True, m), zeros)
    lax.fori_loop(7, 9, lambda v, m: slope_group(v, ref_right, 7, False, m), zeros)

    rows_f[...] = jnp.zeros_like(rows_f)
    rows_s[...] = jnp.zeros_like(rows_s)
    rows8 = row_ids((8, 1)).astype(F32)
    for k in range(3):
        sums = [zeros] * 12
        for v in range(1 + 2 * k, 5 + 2 * k):
            weight = 1.0 - jnp.abs((8 * v - HALO - ELEM * k) + 0.5 + rows8) * (1.0 / ELEM)
            square = weight * weight
            if v < 3:
                weight, square = weight * low_flag, square * low_flag
            if v >= 7:
                weight, square = weight * high_flag, square * high_flag
            for n in range(12):
                sums[n] = sums[n] + (weight if n < 6 else square) * layers[v - 1, n]
        for n in range(6):
            at = k * 6 + n
            rows_f[at : at + 1] = jnp.sum(sums[n], axis=0, keepdims=True)
            rows_s[at : at + 1] = jnp.sum(sums[6 + n], axis=0, keepdims=True)
    force = dot(rows_f[...], over_y[...]) * (1.0 / 12)
    stiffness = dot(rows_s[...], over_y2[...]) * (1.0 / 144)
    shape24 = (24, LANES)
    rows24 = row_ids(shape24)
    lanes24 = lane_ids(shape24)
    direction = force / (stiffness + LEVENBERG)
    direction = jnp.where(rows24 < 12, direction, direction * high_flag)
    held = jnp.where(lanes24 < 8, direction, 0.0)
    owned = jnp.where(rows24 < 12, held, 0.0)
    descent = jnp.sum(force * owned)
    length = jnp.sum(owned * owned)
    rows_f[...] = dot(held, along_y[...])
    curved = zeros
    for v in range(3, 7):
        k = (v - 3) // 2
        share = (8.0 * ((v - 3) % 2) + 0.5 + rows8) * (1.0 / ELEM)
        field = []
        for n in range(6):
            near = rows_f[k * 6 + n : k * 6 + n + 1]
            far = rows_f[k * 6 + 6 + n : k * 6 + 7 + n]
            field.append(near + share * (far - near))
        row = 8 * (v - 3)
        for e in range(2):
            if e == 0:
                move = [field[2 * c] + (field[2 * c + 1] - field[2 * c]) * (1.0 / 32) for c in range(3)]
                gain = [(field[2 * c + 1] - field[2 * c]) * (1.0 / 16) for c in range(3)]
            else:
                move = [field[2 * c + 1] * (31.0 / 32) for c in range(3)]
                gain = [field[2 * c + 1] * (-1.0 / 16) for c in range(3)]
            for j in range(16):
                three = [slopes[c, 16 * e + j, row : row + 8] for c in range(3)]
                projected = (three[0] * move[0] + three[1] * move[1]) + three[2] * move[2]
                curved = curved + projected * projected
                if j < 15:
                    move = [m + g for m, g in zip(move, gain)]
    curvature = jnp.sum(curved) * (1.0 / 144)
    misfit = jnp.sum(misfit)
    line = jnp.sum(jnp.where(pick, direction[0:16], 0.0), axis=0, keepdims=True)
    line_lanes = lane_ids((1, LANES))
    for at, value in ((96, descent), (97, length), (98, curvature), (99, misfit)):
        line = jnp.where(line_lanes == at, value, line)
    block_out[...] = jnp.broadcast_to(line, (tiles, LANES))
    if last:
        residual_out[...] = residuals[pl.ds(place[1] * 8, 8)]


def iteration(tiles, first, last, place, motion, received, targets, cor, tables):
    vmem = pl.BlockSpec(memory_space=pltpu.VMEM)
    args = [place, motion] + ([] if first else [received]) + [*targets, cor, *tables]
    in_specs = [pl.BlockSpec(memory_space=pltpu.SMEM)] + [vmem] * (len(args) - 1)
    in_specs[-5] = pl.BlockSpec(memory_space=pl.ANY)
    shapes = [
        jax.ShapeDtypeStruct((tiles, LANES), F32),
        jax.ShapeDtypeStruct((8, LANES), F32),
    ]
    scratch = [
        pltpu.VMEM((GROUPS, 2, 17, 4, 8, LANES), F32),
        pltpu.VMEM((6 * FRAME, LANES), F32),
        pltpu.VMEM((SLAB + 4, FRAME, LANES), F32),
        pltpu.VMEM((3, SLAB, ROWS, LANES), F32),
        pltpu.VMEM((8, 12, 8, LANES), F32),
        pltpu.VMEM((24, LANES), F32),
        pltpu.VMEM((24, LANES), F32),
        pltpu.VMEM((tiles + 24, LANES), F32),
    ]
    if last:
        shapes.append(jax.ShapeDtypeStruct((8, ROWS, LANES), F32))
        scratch.append(pltpu.VMEM((SLAB, ROWS, LANES), F32))
    scratch.append(pltpu.SemaphoreType.DMA((GROUPS,)))
    return pl.pallas_call(
        functools.partial(iteration_body, tiles, first, last),
        out_shape=shapes,
        in_specs=in_specs,
        out_specs=[vmem] * len(shapes),
        scratch_shapes=scratch,
        cost_estimate=pl.CostEstimate(flops=20000000, bytes_accessed=9000000, transcendentals=0),
        name="iteration",
        compiler_params=pltpu.CompilerParams(vmem_limit_bytes=48 * 2**20),
    )(*args)


def finish_body(tiles, place, motion, got_1, got_2, got_3, ids, displacement, misfits, padded):
    now = updated_motion(motion, got_3, place[0], tiles, padded)
    shape = (8, LANES)
    component = (lane_ids(shape) // 16) % 3
    mine = jnp.where(component == row_ids(shape), jnp.broadcast_to(now[1:2], shape), 0.0)
    mine = jnp.where(lane_ids(shape) < 96, mine, 0.0)
    chooser = jnp.where(ids[...] == lane_ids((LANES, LANES)), 1.0, 0.0)
    placed = dot(mine, chooser)
    displacement[...] = placed[0:3, 0:32]
    for n, got in enumerate((got_1, got_2, got_3)):
        total = jnp.sum(got[...], axis=0, keepdims=True)
        misfits[:, n : n + 1] = total[:, 99:100] * (1.0 / VOXELS)


def finish(tiles, place, motion, got, ids):
    vmem = pl.BlockSpec(memory_space=pltpu.VMEM)
    return pl.pallas_call(
        functools.partial(finish_body, tiles),
        out_shape=[jax.ShapeDtypeStruct((3, 32), F32), jax.ShapeDtypeStruct((1, 3), F32)],
        in_specs=[pl.BlockSpec(memory_space=pltpu.SMEM)] + [vmem] * 5,
        out_specs=[vmem] * 2,
        scratch_shapes=[pltpu.VMEM((tiles + 24, LANES), F32)],
        name="finish",
    )(place, motion, *got, ids)


def from_behind(block, axis, distance):
    devices = range(lax.axis_size(axis))
    return lax.ppermute(block, axis, [(i - distance, i) for i in devices if i - distance in devices])


def ring(block, distance):
    peers = lax.axis_size("depth")
    return lax.ppermute(block, "depth", [((i + distance) % peers, i) for i in range(peers)])


def local(reference_image, deformed_image, offsets, node_ids, start_motion):
    tiles = lax.axis_size("tile")
    tile = lax.axis_index("tile")
    depth = lax.axis_index("depth")
    place = jnp.stack([tile, depth]).astype(jnp.int32)
    tables = [jnp.asarray(table) for table in constants()]

    deformed = [deformed_image] + [ring(deformed_image, n) for n in (1, 2, 3)]
    targets = [reference_image] + [ring(reference_image, n) for n in (1, 2, 3)]

    mine = offsets[:, 0, ::ELEM, :].astype(F32).reshape(6, LANES)
    other = ring(mine, 2)
    upper = depth >= 2
    shifts = jnp.concatenate([jnp.where(upper, other, mine), jnp.where(upper, mine, other)], axis=0)

    local_ids = jnp.transpose(node_ids % 32, (1, 0, 2))
    id_line = jnp.broadcast_to(local_ids[:, None], (2, 3, 2, 8)).reshape(96)
    id_line = jnp.concatenate([id_line, jnp.full((32,), -1, jnp.int32)])
    chooser = (id_line[:, None] == jnp.arange(32, dtype=jnp.int32)[None, :]).astype(F32)
    part = (jnp.arange(LANES, dtype=jnp.int32) // 16) % 3
    line = jnp.sum(chooser * jnp.take(start_motion, part, axis=0), axis=1)[None]
    beyond = from_behind(line, "tile", -2)

    extra = jnp.concatenate([shifts, line, jnp.zeros((HALO - 13, LANES), F32)], axis=0)
    full, low, high = pack(place, deformed, HALO, extra)
    left = from_behind(high, "tile", 1)
    right = from_behind(low, "tile", -1)
    motion = jnp.concatenate(
        [left[SLAB, 12:13], line, right[SLAB, 12:13], beyond, jnp.zeros((4, LANES), F32)], axis=0
    )
    cor = corner_images(tiles, place, full, left, right, extra)

    target_own, target_low, target_high = pack(place, targets, ELEM)
    target_left = from_behind(target_high, "tile", 1)
    target_right = from_behind(target_low, "tile", -1)
    targets = (target_left, target_own, target_right)

    received = None
    got = []
    for number in range(ITERS):
        last = number == ITERS - 1
        outs = iteration(tiles, number == 0, last, place, motion, received, targets, cor, tables)
        block, motion = outs[:2]
        received = lax.all_to_all(block, "tile", 0, 0, tiled=True)
        got.append(received)
    displacement, misfits = finish(tiles, place, motion, got, id_line[:, None])
    return displacement, misfits.reshape(3), outs[2]


def solution(mesh):
    in_specs = (
        P("depth", "tile", None),
        P("depth", "tile", None),
        P(None, "depth", "tile", None),
        P(None, "tile", None),
        P(None, "tile"),
    )
    out_specs = (P(None, "tile"), P(), P("depth", "tile", None))
    return jax.shard_map(local, mesh=mesh, in_specs=in_specs, out_specs=out_specs, check_vma=False)
```

```python
import functools

import jax
import jax.numpy as jnp
from jax import lax
from jax.experimental import pallas as pl
from jax.experimental.pallas import tpu as pltpu
from jax.sharding import PartitionSpec as P

ELEM = 16
ITERS = 3
SLAB = 32
ROWS = 32
LANES = 128
HALO = 24
FRAME = ROWS + 2 * HALO
GROUPS = FRAME // 8
LEVENBERG = 0.1 * ELEM**3
VOXELS = 8388608.0
F32 = jnp.float32

highest = lax.Precision.HIGHEST


def dot(left, right):
    return jnp.dot(left, right, precision=highest, preferred_element_type=F32)


def lane_ids(shape):
    return lax.broadcasted_iota(jnp.int32, shape, 1)


def row_ids(shape):
    return lax.broadcasted_iota(jnp.int32, shape, 0)


def along_y_table(shape, lane_axis):
    y = lax.broadcasted_iota(jnp.int32, shape, 1 - lane_axis).astype(F32) + 0.5
    places = (lax.broadcasted_iota(jnp.int32, shape, lane_axis) % 8 * ELEM).astype(F32)
    return jnp.maximum(1.0 - jnp.abs(y - places) * (1.0 / ELEM), 0.0)


def along_x_table():
    shape = (FRAME, 64)
    row = row_ids(shape).astype(F32) + (0.5 - HALO)
    column = lane_ids(shape)
    node = 2 * (column // 16 - 1) + column % 16 // 6
    hats = jnp.maximum(1.0 - jnp.abs(row - (node * ELEM).astype(F32)) * (1.0 / ELEM), 0.0)
    return [jnp.where((column % 16 < 12) & (column % 16 % 6 == n), hats, 0.0) for n in range(6)]


def prepare_body(offsets, far_ids, far_motion, *refs):
    lines, chooser, along_x, along_y, over_y, over_y2 = refs[:6]
    held, node_ids, start_motion, sem = refs[6:]
    nodes = [
        pltpu.make_async_copy(far_ids, node_ids, sem.at[6]),
        pltpu.make_async_copy(far_motion, start_motion, sem.at[7]),
    ]
    picked = [
        pltpu.make_async_copy(
            offsets.at[c, 0, pl.ds(ELEM * ex, 8)], held.at[2 * c + ex], sem.at[2 * c + ex]
        )
        for c in range(3)
        for ex in range(2)
    ]
    for copy in nodes + picked:
        copy.start()
    for copy in nodes:
        copy.wait()
    shape = (8, LANES)
    lanes = lane_ids(shape)
    eight = jnp.where(lanes % 8 == row_ids(shape), 1.0, 0.0)
    ids = jnp.zeros((1, LANES), F32)
    lanes1 = lane_ids((1, LANES))
    group = lanes1 // 8
    for k in range(2):
        for a in range(2):
            wide = dot((node_ids[a, k : k + 1] % 32).astype(F32), eight)
            ids = jnp.where((group // 6 == k) & (group % 2 == a), wide, ids)
    ids = jnp.where(lanes1 < 96, ids, -1.0)
    chosen = jnp.where(row_ids((32, LANES)).astype(F32) == ids, 1.0, 0.0)
    chooser[...] = chosen
    taken = dot(start_motion[...], chosen)
    component = (lane_ids((3, LANES)) // 16) % 3
    line = jnp.sum(
        jnp.where(component == row_ids((3, LANES)), taken, 0.0), axis=0, keepdims=True
    )
    square = (LANES, LANES)
    along_y[...] = along_y_table(square, 0)
    table = along_y_table(square, 1)
    over_y[...] = table
    over_y2[...] = table * table
    for n, hats in enumerate(along_x_table()):
        along_x[n * FRAME : (n + 1) * FRAME] = hats
    lines[...] = jnp.broadcast_to(line, shape)
    for n, copy in enumerate(picked):
        copy.wait()
        lines[n : n + 1] = held[n, 0:1].astype(F32)


def prepare(offsets, node_ids, start_motion):
    vmem = pl.BlockSpec(memory_space=pltpu.VMEM)
    outside = pl.BlockSpec(memory_space=pltpu.HBM)
    shapes = ((8, LANES), (32, LANES), (6 * FRAME, 64)) + ((LANES, LANES),) * 3
    return pl.pallas_call(
        prepare_body,
        out_shape=[jax.ShapeDtypeStruct(shape, F32) for shape in shapes],
        in_specs=[outside] * 3,
        out_specs=[vmem] * len(shapes),
        scratch_shapes=[
            pltpu.VMEM((6, 8, LANES), jnp.int32),
            pltpu.VMEM(node_ids.shape, jnp.int32),
            pltpu.VMEM(start_motion.shape, F32),
            pltpu.SemaphoreType.DMA((8,)),
        ],
        name="prepare",
        compiler_params=pltpu.CompilerParams(vmem_limit_bytes=2 * 2**20),
    )(offsets, node_ids, start_motion)


def pack_body(*refs):
    both = refs[:4]
    lines, other, beyond, far, far_target, near, near_target, extra = refs[4:]
    depth = lax.axis_index("depth")
    odd = lax.rem(lax.axis_index("tile"), 2)
    for step in range(4):
        planes = pl.ds(lax.rem(depth + step, 4) * 8, 8)
        for part, odds in ((far, odd), (near, 1 - odd)):
            rows = pl.ds(pl.multiple_of(8 * odds, 8), HALO)
            part[planes] = both[step][0:8, rows]
        for part, odds in ((far_target, odd), (near_target, 1 - odd)):
            rows = pl.ds(pl.multiple_of(16 * odds, 8), ELEM)
            part[planes] = both[step][8:16, rows]
    upper = depth >= 2
    mine, given = lines[0:6], other[0:6]
    extra[...] = jnp.zeros_like(extra)
    extra[0:6] = jnp.where(upper, given, mine)
    extra[6:12] = jnp.where(upper, mine, given)
    extra[12:13] = lines[6:7]
    extra[13:14] = beyond[6:7]
    far[SLAB] = extra[...]
    near[SLAB] = extra[...]


def pack(*args):
    sides = (SLAB + 1, HALO, LANES)
    target_sides = (SLAB, ELEM, LANES)
    shapes = (sides, target_sides, sides, target_sides, (HALO, LANES))
    vmem = pl.BlockSpec(memory_space=pltpu.VMEM)
    return pl.pallas_call(
        pack_body,
        out_shape=[jax.ShapeDtypeStruct(shape, F32) for shape in shapes],
        in_specs=[vmem] * len(args),
        out_specs=[vmem] * len(shapes),
        cost_estimate=pl.CostEstimate(flops=0, bytes_accessed=2000000, transcendentals=0),
        name="pack",
        compiler_params=pltpu.CompilerParams(vmem_limit_bytes=4 * 2**20),
    )(*args)


def corner_body(tiles, own, one, two, three, far, near, extra, *refs):
    chunk, motion, source, shifted, table = refs
    tile = lax.axis_index("tile")
    depth = lax.axis_index("depth")
    odd = lax.rem(tile, 2)
    motion[...] = jnp.zeros_like(motion)
    motion[1:2] = extra[12:13]
    motion[3:4] = extra[13:14]
    motion[pl.ds(2 * odd, 1)] = far[SLAB, 12:13]
    motion[pl.ds(2 - 2 * odd, 1)] = near[SLAB, 12:13]
    zero = jnp.zeros((2, FRAME + 16, LANES), F32)
    source[0:2] = zero
    source[SLAB + 2 : SLAB + 4] = zero
    edge = jnp.zeros((SLAB, 8, LANES), F32)
    source[2 : SLAB + 2, 0:8] = edge
    source[2 : SLAB + 2, 8 + FRAME : 16 + FRAME] = edge
    for part, right in ((far, odd), (near, 1 - odd)):
        rows = pl.ds(pl.multiple_of(8 + (HALO + ROWS) * right, 8), HALO)
        source[2 : SLAB + 2, rows] = part[0:SLAB]
    for step, piece in enumerate((own, one, two, three)):
        start = lax.rem(depth + step, 4) * 8
        source[pl.ds(start + 2, 8), 8 + HALO : 8 + HALO + ROWS] = piece[0:8]
    for e in range(2):
        for c in range(3):
            for which in range(2):
                at = e * 6 + c * 2 + which
                row = (e * 6 + which) * 3 + c
                table[row + 6 : row + 7] = extra[at : at + 1]
                table[pl.ds(row + 12 * odd, 1)] = far[SLAB, at : at + 1]
                table[pl.ds(row + 12 - 12 * odd, 1)] = near[SLAB, at : at + 1]

    shape = (8, LANES)
    lanes = lane_ids(shape)

    def group(v, carry):
        ex = (v + 1) // 2
        outside = ((tile == 0) & (v < 3)) | ((tile == tiles - 1) & (v >= 7))
        inside = jnp.where(outside, 0.0, 1.0).astype(F32)
        for e in range(2):
            offs = [
                jnp.broadcast_to(table[pl.ds((e * 6 + ex) * 3 + c, 1)], shape) for c in range(3)
            ]
            base = lanes + offs[2].astype(jnp.int32)
            picks = []
            for s in range(2):
                at = base + s
                good = jnp.where((at >= 0) & (at < LANES), inside, 0.0)
                picks.append((jnp.clip(at, 0, LANES - 1), good))
            for p in range(20):
                for half in range(2):
                    block = source[16 * e + p, pl.ds(8 * v + 6 + 4 * half, 8)]
                    for s in range(2):
                        index, good = picks[s]
                        taken = jnp.take_along_axis(block, index, axis=1, mode="promise_in_bounds")
                        shifted[s, p, 4 * half : 4 * half + 8] = taken * good
            is_x = [offs[1] == float(o) for o in (-2, -1, 0)]
            is_z = [offs[0] == float(o) for o in (-2, -1, 0)]
            window = []
            for p in range(20):
                corners = []
                for sx in range(2):
                    for sy in range(2):
                        rows = [shifted[sy, p, sx + o : sx + o + 8] for o in range(4)]
                        corners.append(
                            jnp.where(
                                is_x[0],
                                rows[0],
                                jnp.where(is_x[1], rows[1], jnp.where(is_x[2], rows[2], rows[3])),
                            )
                        )
                window.append(corners)
                if p >= 3:
                    c00, c01, c10, c11 = [
                        jnp.where(
                            is_z[0],
                            window[p - 3][n],
                            jnp.where(
                                is_z[1],
                                window[p - 2][n],
                                jnp.where(is_z[2], window[p - 1][n], window[p][n]),
                            ),
                        )
                        for n in range(4)
                    ]
                    chunk[v, e, p - 3, 0] = c00
                    chunk[v, e, p - 3, 1] = c01 - c00
                    chunk[v, e, p - 3, 2] = c10 - c00
                    chunk[v, e, p - 3, 3] = (c11 - c10) - (c01 - c00)
        return carry

    lax.fori_loop(0, GROUPS, group, 0)


def corner_images(tiles, *args):
    vmem = pl.BlockSpec(memory_space=pltpu.VMEM)
    shape = (GROUPS, 2, 17, 4, 8, LANES)
    return pl.pallas_call(
        functools.partial(corner_body, tiles),
        out_shape=[
            jax.ShapeDtypeStruct(size, F32)
            for size in (shape, (8, LANES))
        ],
        in_specs=[vmem] * len(args),
        out_specs=[vmem] * 2,
        scratch_shapes=[
            pltpu.VMEM((SLAB + 4, FRAME + 16, LANES), F32),
            pltpu.VMEM((2, 20, 16, LANES), F32),
            pltpu.VMEM((40, LANES), F32),
        ],
        cost_estimate=pl.CostEstimate(flops=10000000, bytes_accessed=9000000, transcendentals=0),
        name="corners",
        compiler_params=pltpu.CompilerParams(vmem_limit_bytes=12 * 2**20),
    )(*args)


def updated_motion(motion, received, tile, tiles, padded):
    padded[...] = jnp.zeros_like(padded)
    padded[8 : 8 + tiles] = received[...]
    total = jnp.sum(received[...], axis=0, keepdims=True)
    descent = total[:, 96:97]
    length = total[:, 97:98]
    curvature = total[:, 98:99]
    step = descent / (curvature + LEVENBERG * length)
    near = padded[pl.ds(7 + tile, 8)]
    return motion[...] - step * near


def iteration_body(tiles, first, last, *refs):
    refs = list(refs)
    motion = refs.pop(0)
    received = None if first else refs.pop(0)
    if first:
        pieces, refs = refs[:6], refs[6:]
    else:
        target = refs.pop(0)
    cors, along_x, along_y, over_y, over_y2, block_out, motion_out = refs[:7]
    refs = refs[7:]
    if first:
        target = refs.pop(0)
    residual_out = refs.pop(0) if last else None
    wide, warped, slopes, layers, rows_f, rows_s, padded = refs[:7]
    residuals = refs[7] if last else None

    tile = lax.axis_index("tile")
    if first:
        depth = lax.axis_index("depth")
        odd = lax.rem(tile, 2)
        for step, piece in enumerate(pieces[:4]):
            start = lax.rem(depth + step, 4) * 8
            target[pl.ds(start, 8), ELEM : ELEM + ROWS] = piece[8:16]
        for part, right in ((pieces[4], odd), (pieces[5], 1 - odd)):
            target[:, pl.ds(pl.multiple_of((ELEM + ROWS) * right, 8), ELEM)] = part[...]
    low_flag = jnp.where(tile > 0, 1.0, 0.0).astype(F32)
    high_flag = jnp.where(tile < tiles - 1, 1.0, 0.0).astype(F32)
    now = motion[...] if first else updated_motion(motion, received, tile, tiles, padded)
    motion_out[...] = now
    shape16 = (16, LANES)
    pick = (lane_ids(shape16) // 8 == row_ids(shape16)) & (row_ids(shape16) < 12)
    spread = jnp.concatenate(
        [jnp.where(pick, jnp.broadcast_to(now[n : n + 1], shape16), 0.0) for n in range(4)], axis=0
    )
    wide[...] = dot(along_x[...], dot(spread, along_y[...]))

    zero = jnp.zeros((2, FRAME, LANES), F32)
    warped[0:2] = zero
    warped[SLAB + 2 : SLAB + 4] = zero

    def warp(v, carry):
        at = pl.ds(pl.multiple_of(8 * v, 8), 8)
        near = [wide[pl.ds(pl.multiple_of(2 * c * FRAME + 8 * v, 8), 8)] for c in range(3)]
        far = [wide[pl.ds(pl.multiple_of((2 * c + 1) * FRAME + 8 * v, 8), 8)] for c in range(3)]
        for e in range(2):
            if e == 0:
                move = [n + (f - n) * (1.0 / 32) for n, f in zip(near, far)]
                gain = [(f - n) * (1.0 / 16) for n, f in zip(near, far)]
            else:
                move = [f * (31.0 / 32) for f in far]
                gain = [f * (-1.0 / 16) for f in far]
            plane = [cors[v, e, 0, n] for n in range(4)]
            for j in range(16):
                above = [cors[v, e, j + 1, n] for n in range(4)]
                mz, mx, my = move
                here = (plane[0] + my * plane[1]) + mx * (plane[2] + my * plane[3])
                there = (above[0] + my * above[1]) + mx * (above[2] + my * above[3])
                warped[2 + 16 * e + j, at] = here + mz * (there - here)
                plane = above
                if j < 15:
                    move = [m + g for m, g in zip(move, gain)]
        return carry

    lax.fori_loop(0, GROUPS, warp, 0)

    shape = (8, LANES)
    lanes = lane_ids(shape)
    ahead_1 = jnp.where(lanes < LANES - 1, 8.0, 0.0)
    behind_1 = jnp.where(lanes > 0, 8.0, 0.0)
    ahead_2 = jnp.where(lanes < LANES - 2, 1.0, 0.0)
    behind_2 = jnp.where(lanes > 1, 1.0, 0.0)
    zeros = jnp.zeros(shape, F32)

    def slope_group(v, own, misfit):
        at = pl.ds(pl.multiple_of(8 * v, 8), 8)
        row = pl.multiple_of(8 * (v - 3), 8)
        goal = pl.ds(pl.multiple_of(8 * (v - 1), 8), 8)
        planes = [warped[n, at] for n in range(4)]
        for e in range(2):
            first_sum = [zeros] * 3
            second_sum = [zeros] * 3
            squares_0 = [zeros] * 3
            squares_1 = [zeros] * 3
            for j in range(16):
                z = 16 * e + j
                planes.append(warped[z + 4, at])
                mid = planes[2]
                slope_z = 8.0 * (planes[3] - planes[1]) - (planes[4] - planes[0])
                planes = planes[1:]
                up_1 = warped[z + 2, pl.ds(8 * v + 1, 8)]
                up_2 = warped[z + 2, pl.ds(8 * v + 2, 8)]
                down_1 = warped[z + 2, pl.ds(8 * v - 1, 8)]
                down_2 = warped[z + 2, pl.ds(8 * v - 2, 8)]
                slope_x = 8.0 * (up_1 - down_1) - (up_2 - down_2)
                slope_y = (
                    ahead_1 * pltpu.roll(mid, LANES - 1, 1) - behind_1 * pltpu.roll(mid, 1, 1)
                ) - (ahead_2 * pltpu.roll(mid, LANES - 2, 1) - behind_2 * pltpu.roll(mid, 2, 1))
                residual = mid - target[z, goal]
                three = (slope_z, slope_x, slope_y)
                if own:
                    misfit = misfit + residual * residual
                    for c in range(3):
                        slopes[c, z, pl.ds(row, 8)] = three[c]
                    if last:
                        residuals[z, pl.ds(row, 8)] = residual
                weight = 1.0 - (j + 0.5) / 16.0
                for c in range(3):
                    first_sum[c] = first_sum[c] + three[c] * residual
                    second_sum[c] = second_sum[c] + first_sum[c]
                    square = three[c] * three[c]
                    squares_0[c] = squares_0[c] + (weight * weight) * square
                    if e == 0:
                        squares_1[c] = squares_1[c] + ((1.0 - weight) ** 2) * square
            for c in range(3):
                falling = (second_sum[c] - 0.5 * first_sum[c]) * (1.0 / 16)
                if e == 0:
                    layers[v - 1, 2 * c] = falling
                    layers[v - 1, 2 * c + 1] = first_sum[c] - falling
                    layers[v - 1, 6 + 2 * c] = squares_0[c]
                    layers[v - 1, 6 + 2 * c + 1] = squares_1[c]
                else:
                    layers[v - 1, 2 * c + 1] += falling
                    layers[v - 1, 6 + 2 * c + 1] += squares_0[c]
        return misfit

    lax.fori_loop(1, 3, lambda v, m: slope_group(v, False, m), zeros)
    misfit = lax.fori_loop(3, 7, lambda v, m: slope_group(v, True, m), zeros)
    lax.fori_loop(7, 9, lambda v, m: slope_group(v, False, m), zeros)

    rows_f[...] = jnp.zeros_like(rows_f)
    rows_s[...] = jnp.zeros_like(rows_s)
    rows8 = row_ids((8, 1)).astype(F32)
    for k in range(3):
        sums = [zeros] * 12
        for v in range(1 + 2 * k, 5 + 2 * k):
            weight = 1.0 - jnp.abs((8 * v - HALO - ELEM * k) + 0.5 + rows8) * (1.0 / ELEM)
            square = weight * weight
            if v < 3:
                weight, square = weight * low_flag, square * low_flag
            if v >= 7:
                weight, square = weight * high_flag, square * high_flag
            for n in range(12):
                sums[n] = sums[n] + (weight if n < 6 else square) * layers[v - 1, n]
        for n in range(6):
            at = k * 6 + n
            rows_f[at : at + 1] = jnp.sum(sums[n], axis=0, keepdims=True)
            rows_s[at : at + 1] = jnp.sum(sums[6 + n], axis=0, keepdims=True)
    force = dot(rows_f[...], over_y[...]) * (1.0 / 12)
    stiffness = dot(rows_s[...], over_y2[...]) * (1.0 / 144)
    shape24 = (24, LANES)
    rows24 = row_ids(shape24)
    lanes24 = lane_ids(shape24)
    direction = force / (stiffness + LEVENBERG)
    direction = jnp.where(rows24 < 12, direction, direction * high_flag)
    held = jnp.where(lanes24 < 8, direction, 0.0)
    owned = jnp.where(rows24 < 12, held, 0.0)
    descent = jnp.sum(force * owned)
    length = jnp.sum(owned * owned)
    rows_f[...] = dot(held, along_y[...])
    curved = zeros
    for v in range(3, 7):
        k = (v - 3) // 2
        share = (8.0 * ((v - 3) % 2) + 0.5 + rows8) * (1.0 / ELEM)
        field = []
        for n in range(6):
            near = rows_f[k * 6 + n : k * 6 + n + 1]
            far = rows_f[k * 6 + 6 + n : k * 6 + 7 + n]
            field.append(near + share * (far - near))
        row = 8 * (v - 3)
        for e in range(2):
            if e == 0:
                move = [field[2 * c] + (field[2 * c + 1] - field[2 * c]) * (1.0 / 32) for c in range(3)]
                gain = [(field[2 * c + 1] - field[2 * c]) * (1.0 / 16) for c in range(3)]
            else:
                move = [field[2 * c + 1] * (31.0 / 32) for c in range(3)]
                gain = [field[2 * c + 1] * (-1.0 / 16) for c in range(3)]
            for j in range(16):
                three = [slopes[c, 16 * e + j, row : row + 8] for c in range(3)]
                projected = (three[0] * move[0] + three[1] * move[1]) + three[2] * move[2]
                curved = curved + projected * projected
                if j < 15:
                    move = [m + g for m, g in zip(move, gain)]
    curvature = jnp.sum(curved) * (1.0 / 144)
    misfit = jnp.sum(misfit)
    line = jnp.sum(jnp.where(pick, direction[0:16], 0.0), axis=0, keepdims=True)
    line_lanes = lane_ids((1, LANES))
    for at, value in ((96, descent), (97, length), (98, curvature), (99, misfit)):
        line = jnp.where(line_lanes == at, value, line)
    block_out[...] = jnp.broadcast_to(line, (tiles, LANES))
    if last:
        residual_out[...] = residuals[pl.ds(lax.axis_index("depth") * 8, 8)]


def iteration(tiles, first, last, motion, received, target, cor, tables):
    vmem = pl.BlockSpec(memory_space=pltpu.VMEM)
    args = [motion] + ([] if first else [received]) + [*target, cor, *tables]
    shapes = [
        jax.ShapeDtypeStruct((tiles, LANES), F32),
        jax.ShapeDtypeStruct((8, LANES), F32),
    ]
    scratch = [
        pltpu.VMEM((6 * FRAME, LANES), F32),
        pltpu.VMEM((SLAB + 4, FRAME, LANES), F32),
        pltpu.VMEM((3, SLAB, ROWS, LANES), F32),
        pltpu.VMEM((8, 12, 8, LANES), F32),
        pltpu.VMEM((24, LANES), F32),
        pltpu.VMEM((24, LANES), F32),
        pltpu.VMEM((tiles + 24, LANES), F32),
    ]
    if first:
        shapes.append(jax.ShapeDtypeStruct((SLAB, ROWS + 2 * ELEM, LANES), F32))
    if last:
        shapes.append(jax.ShapeDtypeStruct((8, ROWS, LANES), F32))
        scratch.append(pltpu.VMEM((SLAB, ROWS, LANES), F32))
    return pl.pallas_call(
        functools.partial(iteration_body, tiles, first, last),
        out_shape=shapes,
        in_specs=[vmem] * len(args),
        out_specs=[vmem] * len(shapes),
        scratch_shapes=scratch,
        cost_estimate=pl.CostEstimate(flops=20000000, bytes_accessed=9000000, transcendentals=0),
        name="iteration",
        compiler_params=pltpu.CompilerParams(vmem_limit_bytes=16 * 2**20),
    )(*args)


def finish_body(tiles, motion, got_1, got_2, got_3, chooser, displacement, misfits, padded):
    now = updated_motion(motion, got_3, lax.axis_index("tile"), tiles, padded)
    shape = (8, LANES)
    component = (lane_ids(shape) // 16) % 3
    mine = jnp.where(component == row_ids(shape), jnp.broadcast_to(now[1:2], shape), 0.0)
    mine = jnp.where(lane_ids(shape) < 96, mine, 0.0)
    placed = lax.dot_general(
        mine, chooser[...], (((1,), (1,)), ((), ())), precision=highest, preferred_element_type=F32
    )
    displacement[...] = placed[0:3]
    for n, got in enumerate((got_1, got_2, got_3)):
        total = jnp.sum(got[...], axis=0, keepdims=True)
        misfits[:, n : n + 1] = total[:, 99:100] * (1.0 / VOXELS)


def finish(tiles, motion, got, chooser):
    vmem = pl.BlockSpec(memory_space=pltpu.VMEM)
    return pl.pallas_call(
        functools.partial(finish_body, tiles),
        out_shape=[jax.ShapeDtypeStruct((3, 32), F32), jax.ShapeDtypeStruct((1, 3), F32)],
        in_specs=[vmem] * 5,
        out_specs=[vmem] * 2,
        scratch_shapes=[pltpu.VMEM((tiles + 24, LANES), F32)],
        name="finish",
        compiler_params=pltpu.CompilerParams(vmem_limit_bytes=2**20),
    )(motion, *got, chooser)


def from_behind(block, axis, distance):
    devices = range(lax.axis_size(axis))
    return lax.ppermute(block, axis, [(i - distance, i) for i in devices if i - distance in devices])


def swap(block, first):
    pairs = [(i, i + 1) for i in range(first, lax.axis_size("tile") - 1, 2)]
    return lax.ppermute(block, "tile", pairs + [(j, i) for i, j in pairs])


def ring(block, distance):
    peers = lax.axis_size("depth")
    return lax.ppermute(block, "depth", [((i + distance) % peers, i) for i in range(peers)])


def local(reference_image, deformed_image, offsets, node_ids, start_motion):
    tiles = lax.axis_size("tile")
    both = jnp.concatenate([deformed_image, reference_image], axis=0)
    both = [both] + [ring(both, n) for n in (1, 2, 3)]
    lines, chooser, *tables = prepare(offsets, node_ids, start_motion)
    other = ring(lines, 2)
    beyond = from_behind(lines, "tile", -2)
    far, far_target, near, near_target, extra = pack(*both, lines, other, beyond)
    far = swap(far, 1)
    near = swap(near, 0)
    far_target = swap(far_target, 1)
    near_target = swap(near_target, 0)
    cor, motion = corner_images(tiles, *both, far, near, extra)
    target = (*both, far_target, near_target)
    received = None
    got = []
    for number in range(ITERS):
        first, last = number == 0, number == ITERS - 1
        outs = iteration(tiles, first, last, motion, received, target, cor, tables)
        block, motion = outs[:2]
        if first:
            target = (outs[2],)
        received = lax.all_to_all(block, "tile", 0, 0, tiled=True)
        got.append(received)
    displacement, misfits = finish(tiles, motion, got, chooser)
    return displacement, misfits.reshape(3), outs[2]


def solution(mesh):
    in_specs = (
        P("depth", "tile", None),
        P("depth", "tile", None),
        P(None, "depth", "tile", None),
        P(None, "tile", None),
        P(None, "tile"),
    )
    out_specs = (P(None, "tile"), P(), P("depth", "tile", None))
    return jax.shard_map(local, mesh=mesh, in_specs=in_specs, out_specs=out_specs, check_vma=False)
```

```python
import functools

import jax
import jax.numpy as jnp
from jax import lax
from jax.experimental import pallas as pl
from jax.experimental.pallas import tpu as pltpu
from jax.sharding import PartitionSpec as P

ELEM = 16
ITERS = 3
SLAB = 32
ROWS = 32
LANES = 128
HALO = 24
FRAME = ROWS + 2 * HALO
GROUPS = FRAME // 8
LEVENBERG = 0.1 * ELEM**3
VOXELS = 8388608.0
F32 = jnp.float32

highest = lax.Precision.HIGHEST


def dot(left, right):
    return jnp.dot(left, right, precision=highest, preferred_element_type=F32)


def split(value, parts):
    pieces = []
    for _ in range(parts):
        piece = value.astype(jnp.bfloat16)
        pieces.append(piece)
        value = value - piece.astype(F32)
    return pieces


def exact_dot(left, tables):
    left = jnp.concatenate(split(left, 3) * len(tables), axis=1)
    right = jnp.concatenate([table for table in tables for _ in range(3)], axis=0)
    return jnp.dot(left, right, preferred_element_type=F32)


def lane_ids(shape):
    return lax.broadcasted_iota(jnp.int32, shape, 1)


def row_ids(shape):
    return lax.broadcasted_iota(jnp.int32, shape, 0)


def along_y_table(shape, lane_axis):
    y = lax.broadcasted_iota(jnp.int32, shape, 1 - lane_axis).astype(F32) + 0.5
    places = (lax.broadcasted_iota(jnp.int32, shape, lane_axis) % 8 * ELEM).astype(F32)
    return jnp.maximum(1.0 - jnp.abs(y - places) * (1.0 / ELEM), 0.0)


def prepare_body(offsets, far_ids, far_motion, *refs):
    lines, chooser, along_y, over_y, over_y2 = refs[:5]
    held, node_ids, start_motion, sem = refs[5:]
    nodes = [
        pltpu.make_async_copy(far_ids, node_ids, sem.at[6]),
        pltpu.make_async_copy(far_motion, start_motion, sem.at[7]),
    ]
    picked = [
        pltpu.make_async_copy(
            offsets.at[c, 0, pl.ds(ELEM * ex, 8)], held.at[2 * c + ex], sem.at[2 * c + ex]
        )
        for c in range(3)
        for ex in range(2)
    ]
    for copy in nodes + picked:
        copy.start()
    for copy in nodes:
        copy.wait()
    shape = (8, LANES)
    lanes = lane_ids(shape)
    eight = jnp.where(lanes % 8 == row_ids(shape), 1.0, 0.0)
    ids = jnp.zeros((1, LANES), F32)
    lanes1 = lane_ids((1, LANES))
    group = lanes1 // 8
    for k in range(2):
        for a in range(2):
            wide = dot((node_ids[a, k : k + 1] % 32).astype(F32), eight)
            ids = jnp.where((group // 6 == k) & (group % 2 == a), wide, ids)
    ids = jnp.where(lanes1 < 96, ids, -1.0)
    chosen = jnp.where(row_ids((32, LANES)).astype(F32) == ids, 1.0, 0.0)
    chooser[...] = chosen
    taken = dot(start_motion[...], chosen)
    component = (lane_ids((3, LANES)) // 16) % 3
    line = jnp.sum(
        jnp.where(component == row_ids((3, LANES)), taken, 0.0), axis=0, keepdims=True
    )
    square = (LANES, LANES)
    along_y[...] = along_y_table(square, 0).astype(jnp.bfloat16)
    table = along_y_table(square, 1)
    over_y[...] = table.astype(jnp.bfloat16)
    over_y2[0], over_y2[1] = split(table * table, 2)
    lines[...] = jnp.broadcast_to(line, shape)
    for n, copy in enumerate(picked):
        copy.wait()
        lines[n : n + 1] = held[n, 0:1].astype(F32)


def prepare(offsets, node_ids, start_motion):
    vmem = pl.BlockSpec(memory_space=pltpu.VMEM)
    outside = pl.BlockSpec(memory_space=pltpu.HBM)
    shapes = [jax.ShapeDtypeStruct((n, LANES), F32) for n in (8, 32)]
    for size in ((LANES, LANES), (LANES, LANES), (2, LANES, LANES)):
        shapes.append(jax.ShapeDtypeStruct(size, jnp.bfloat16))
    return pl.pallas_call(
        prepare_body,
        out_shape=shapes,
        in_specs=[outside] * 3,
        out_specs=[vmem] * len(shapes),
        scratch_shapes=[
            pltpu.VMEM((6, 8, LANES), jnp.int32),
            pltpu.VMEM(node_ids.shape, jnp.int32),
            pltpu.VMEM(start_motion.shape, F32),
            pltpu.SemaphoreType.DMA((8,)),
        ],
        name="prepare",
        compiler_params=pltpu.CompilerParams(vmem_limit_bytes=2 * 2**20),
    )(offsets, node_ids, start_motion)


def pack_body(*refs):
    both = refs[:4]
    lines, other, beyond, far, far_target, near, extra = refs[4:]
    depth = lax.axis_index("depth")
    odd = lax.rem(lax.axis_index("tile"), 2)
    far_rows = pl.ds(pl.multiple_of(8 * odd, 8), HALO)
    near_rows = pl.ds(pl.multiple_of(8 * (1 - odd), 8), HALO)
    for step, piece in enumerate(both):
        planes = pl.ds(lax.rem(depth + step, 4) * 8, 8)
        far[planes] = piece[0:8, far_rows]
        near[planes, :HALO] = piece[0:8, near_rows]
        far_target[planes] = piece[8:16, pl.ds(pl.multiple_of(ELEM * odd, 8), ELEM)]
        near[planes, HALO:] = piece[8:16, pl.ds(pl.multiple_of(ELEM * (1 - odd), 8), ELEM)]
    upper = depth >= 2
    mine, given = lines[0:6], other[0:6]
    extra[...] = jnp.zeros_like(extra)
    extra[0:6] = jnp.where(upper, given, mine)
    extra[6:12] = jnp.where(upper, mine, given)
    extra[12:13] = lines[6:7]
    extra[13:14] = beyond[6:7]
    far[SLAB] = extra[...]
    near[SLAB, :HALO] = extra[...]
    near[SLAB, HALO:] = jnp.zeros((ELEM, LANES), F32)


def pack(*args):
    shapes = (
        (SLAB + 1, HALO, LANES),
        (SLAB, ELEM, LANES),
        (SLAB + 1, HALO + ELEM, LANES),
        (HALO, LANES),
    )
    vmem = pl.BlockSpec(memory_space=pltpu.VMEM)
    return pl.pallas_call(
        pack_body,
        out_shape=[jax.ShapeDtypeStruct(shape, F32) for shape in shapes],
        in_specs=[vmem] * len(args),
        out_specs=[vmem] * len(shapes),
        cost_estimate=pl.CostEstimate(flops=0, bytes_accessed=2000000, transcendentals=0),
        name="pack",
        compiler_params=pltpu.CompilerParams(vmem_limit_bytes=4 * 2**20),
    )(*args)


def near_base(odd):
    return 4 * (1 - odd)


def far_base(odd):
    return 6 * odd


def corner_body(tiles, is_far, own, one, two, three, part, *refs):
    if is_far:
        near, extra, chunk, motion, source, shifted, table = refs
    else:
        extra, chunk, source, shifted, table = refs
    tile = lax.axis_index("tile")
    depth = lax.axis_index("depth")
    odd = lax.rem(tile, 2)
    if is_far:
        motion[...] = jnp.zeros_like(motion)
        motion[1:2] = extra[12:13]
        motion[3:4] = extra[13:14]
        motion[pl.ds(2 * odd, 1)] = part[SLAB, 12:13]
        motion[pl.ds(2 - 2 * odd, 1)] = near[SLAB, 12:13]
    right = odd if is_far else 1 - odd
    base = far_base(odd) if is_far else near_base(odd)
    rows = pl.ds(pl.multiple_of(8 + (HALO + ROWS) * right, 8), HALO)
    source[:, rows] = part[0:SLAB, :HALO]
    for step, piece in enumerate((own, one, two, three)):
        start = lax.rem(depth + step, 4) * 8
        source[pl.ds(start, 8), 8 + HALO : 8 + HALO + ROWS] = piece[0:8]
    for e in range(2):
        for c in range(3):
            for which in range(2):
                at = e * 6 + c * 2 + which
                row = (e * 6 + which) * 3 + c
                table[row + 6 : row + 7] = extra[at : at + 1]
                table[pl.ds(row + 12 * right, 1)] = part[SLAB, at : at + 1]

    shape = (8, LANES)
    lanes = lane_ids(shape)
    zeros = jnp.zeros(shape, F32)

    def group(number, carry):
        v = base + number
        ex = (v + 1) // 2
        outside = ((tile == 0) & (v < 3)) | ((tile == tiles - 1) & (v >= 7))
        inside = jnp.where(outside, 0.0, 1.0).astype(F32)
        for e in range(2):
            offs = [
                jnp.broadcast_to(table[pl.ds((e * 6 + ex) * 3 + c, 1)], shape) for c in range(3)
            ]
            reach = lanes + offs[2].astype(jnp.int32)
            picks = []
            for s in range(2):
                at = reach + s
                good = jnp.where((at >= 0) & (at < LANES), inside, 0.0)
                picks.append((jnp.clip(at, 0, LANES - 1), good))
            is_x = [offs[1] == float(o) for o in (-2, -1, 0)]
            odd_z = (offs[0] == -1.0) | (offs[0] == 1.0)
            high_z = offs[0] >= 0.0
            planes = []
            steps = []
            for p in range(20):
                z = 16 * e + p - 2
                corners = [zeros] * 4
                if 0 <= z < SLAB:
                    for half in range(2):
                        block = source[z, pl.ds(8 * v + 6 + 4 * half, 8)]
                        for s in range(2):
                            index, good = picks[s]
                            taken = jnp.take_along_axis(
                                block, index, axis=1, mode="promise_in_bounds"
                            )
                            shifted[e, s, p, 4 * half : 4 * half + 8] = taken * good
                    corners = []
                    for sx in range(2):
                        for sy in range(2):
                            rows = [shifted[e, sy, p, sx + o : sx + o + 8] for o in range(4)]
                            corners.append(
                                jnp.where(
                                    is_x[0],
                                    rows[0],
                                    jnp.where(
                                        is_x[1], rows[1], jnp.where(is_x[2], rows[2], rows[3])
                                    ),
                                )
                            )
                planes.append(corners)
                if p >= 1:
                    steps.append(
                        [jnp.where(odd_z, planes[p][n], planes[p - 1][n]) for n in range(4)]
                    )
                if p >= 3:
                    c00, c01, c10, c11 = [
                        jnp.where(high_z, steps[p - 1][n], steps[p - 3][n]) for n in range(4)
                    ]
                    along = c01 - c00
                    chunk[number, e, p - 3, 0] = c00
                    chunk[number, e, p - 3, 1] = along
                    chunk[number, e, p - 3, 2] = c10 - c00
                    chunk[number, e, p - 3, 3] = (c11 - c10) - along
        return carry

    lax.fori_loop(0, chunk.shape[0], group, 0)


def corner_images(tiles, is_far, *args):
    vmem = pl.BlockSpec(memory_space=pltpu.VMEM)
    shapes = [(4 if is_far else 6, 2, 17, 4, 8, LANES)] + ([(8, LANES)] if is_far else [])
    return pl.pallas_call(
        functools.partial(corner_body, tiles, is_far),
        out_shape=[jax.ShapeDtypeStruct(shape, F32) for shape in shapes],
        in_specs=[vmem] * len(args),
        out_specs=[vmem] * len(shapes),
        scratch_shapes=[
            pltpu.VMEM((SLAB, FRAME + 16, LANES), F32),
            pltpu.VMEM((2, 2, 20, 16, LANES), F32),
            pltpu.VMEM((40, LANES), F32),
        ],
        cost_estimate=pl.CostEstimate(flops=5000000, bytes_accessed=4000000, transcendentals=0),
        name="corners_far" if is_far else "corners_near",
        compiler_params=pltpu.CompilerParams(vmem_limit_bytes=8 * 2**20),
    )(*args)


def updated_motion(motion, received, tile, tiles, padded):
    padded[...] = jnp.zeros_like(padded)
    padded[8 : 8 + tiles] = received[...]
    total = jnp.sum(received[...], axis=0, keepdims=True)
    descent = total[:, 96:97]
    length = total[:, 97:98]
    curvature = total[:, 98:99]
    step = descent / (curvature + LEVENBERG * length)
    near = padded[pl.ds(7 + tile, 8)]
    return motion[...] - step * near


def iteration_body(tiles, first, last, *refs):
    refs = list(refs)
    motion = refs.pop(0)
    received = None if first else refs.pop(0)
    if first:
        pieces, refs = refs[:6], refs[6:]
    else:
        target = refs.pop(0)
    near_cors, far_cors, along_y, over_y, over_y2, block_out, motion_out = refs[:7]
    refs = refs[7:]
    if first:
        target = refs.pop(0)
    residual_out = refs.pop(0) if last else None
    wide, ends, warped, slopes, layers, rows_f, rows_s, padded = refs[:8]
    residuals = refs[8] if last else None

    tile = lax.axis_index("tile")
    odd = lax.rem(tile, 2)
    if first:
        depth = lax.axis_index("depth")
        for step, piece in enumerate(pieces[:4]):
            start = lax.rem(depth + step, 4) * 8
            target[pl.ds(start, 8), ELEM : ELEM + ROWS] = piece[8:16]
        far = pl.ds(pl.multiple_of((ELEM + ROWS) * odd, 8), ELEM)
        near = pl.ds(pl.multiple_of((ELEM + ROWS) * (1 - odd), 8), ELEM)
        target[:, far] = pieces[4][...]
        target[:, near] = pieces[5][0:SLAB, HALO:]
    low_flag = jnp.where(tile > 0, 1.0, 0.0).astype(F32)
    high_flag = jnp.where(tile < tiles - 1, 1.0, 0.0).astype(F32)
    now = motion[...] if first else updated_motion(motion, received, tile, tiles, padded)
    motion_out[...] = now
    shape16 = (16, LANES)
    pick = (lane_ids(shape16) // 8 == row_ids(shape16)) & (row_ids(shape16) < 12)
    spread = jnp.concatenate(
        [jnp.where(pick, jnp.broadcast_to(now[n : n + 1], shape16), 0.0) for n in range(4)], axis=0
    )
    wide[...] = exact_dot(spread, [along_y[...]])

    zero = jnp.zeros((2, FRAME, LANES), F32)
    warped[0:2] = zero
    warped[SLAB + 2 : SLAB + 4] = zero

    shares = (row_ids((8, LANES)).astype(F32) + 0.5) * (1.0 / ELEM)
    for v in range(GROUPS):
        node = (v + 1) // 2
        lower = 16 * (node // 2) + 6 * (node % 2)
        upper = 16 * ((node + 1) // 2) + 6 * ((node + 1) % 2)
        share = shares + 0.5 * ((v + 1) % 2)
        for n in range(6):
            begin = wide[lower + n : lower + n + 1]
            ends[v, n] = begin + share * (wide[upper + n : upper + n + 1] - begin)

    def warp(cors, base, number, carry):
        v = base + number
        at = pl.ds(pl.multiple_of(8 * v, 8), 8)
        near = [ends[v, 2 * c] for c in range(3)]
        far = [ends[v, 2 * c + 1] for c in range(3)]
        for e in range(2):
            if e == 0:
                move = [n + (f - n) * (1.0 / 32) for n, f in zip(near, far)]
                gain = [(f - n) * (1.0 / 16) for n, f in zip(near, far)]
            else:
                move = [f * (31.0 / 32) for f in far]
                gain = [f * (-1.0 / 16) for f in far]
            plane = [cors[number, e, 0, n] for n in range(4)]
            for j in range(16):
                above = [cors[number, e, j + 1, n] for n in range(4)]
                mz, mx, my = move
                here = (plane[0] + my * plane[1]) + mx * (plane[2] + my * plane[3])
                there = (above[0] + my * above[1]) + mx * (above[2] + my * above[3])
                warped[2 + 16 * e + j, at] = here + mz * (there - here)
                plane = above
                if j < 15:
                    move = [m + g for m, g in zip(move, gain)]
        return carry

    lax.fori_loop(0, 6, functools.partial(warp, near_cors, near_base(odd)), 0)
    lax.fori_loop(0, 4, functools.partial(warp, far_cors, far_base(odd)), 0)

    shape = (8, LANES)
    lanes = lane_ids(shape)
    ahead_1 = jnp.where(lanes < LANES - 1, 8.0, 0.0)
    behind_1 = jnp.where(lanes > 0, 8.0, 0.0)
    ahead_2 = jnp.where(lanes < LANES - 2, 1.0, 0.0)
    behind_2 = jnp.where(lanes > 1, 1.0, 0.0)
    zeros = jnp.zeros(shape, F32)

    def slope_group(v, own, misfit):
        at = pl.ds(pl.multiple_of(8 * v, 8), 8)
        row = pl.multiple_of(8 * (v - 3), 8)
        goal = pl.ds(pl.multiple_of(8 * (v - 1), 8), 8)
        planes = [warped[n, at] for n in range(4)]
        for e in range(2):
            first_sum = [zeros] * 3
            second_sum = [zeros] * 3
            squares_0 = [zeros] * 3
            squares_1 = [zeros] * 3
            squares_2 = [zeros] * 3
            for j in range(16):
                z = 16 * e + j
                planes.append(warped[z + 4, at])
                mid = planes[2]
                slope_z = 8.0 * (planes[3] - planes[1]) - (planes[4] - planes[0])
                planes = planes[1:]
                up_1 = warped[z + 2, pl.ds(8 * v + 1, 8)]
                up_2 = warped[z + 2, pl.ds(8 * v + 2, 8)]
                down_1 = warped[z + 2, pl.ds(8 * v - 1, 8)]
                down_2 = warped[z + 2, pl.ds(8 * v - 2, 8)]
                slope_x = 8.0 * (up_1 - down_1) - (up_2 - down_2)
                slope_y = (
                    ahead_1 * pltpu.roll(mid, LANES - 1, 1) - behind_1 * pltpu.roll(mid, 1, 1)
                ) - (ahead_2 * pltpu.roll(mid, LANES - 2, 1) - behind_2 * pltpu.roll(mid, 2, 1))
                residual = mid - target[z, goal]
                three = (slope_z, slope_x, slope_y)
                if own:
                    misfit = misfit + residual * residual
                    for c in range(3):
                        slopes[c, z, pl.ds(row, 8)] = three[c]
                    if last:
                        residuals[z, pl.ds(row, 8)] = residual
                weight = 1.0 - (j + 0.5) / 16.0
                for c in range(3):
                    first_sum[c] = first_sum[c] + three[c] * residual
                    second_sum[c] = second_sum[c] + first_sum[c]
                    square = three[c] * three[c]
                    if e == 0:
                        squares_0[c] = squares_0[c] + square
                        squares_1[c] = squares_1[c] + squares_0[c]
                        squares_2[c] = squares_2[c] + squares_1[c]
                    else:
                        squares_0[c] = squares_0[c] + (weight * weight) * square
            for c in range(3):
                falling = (second_sum[c] - 0.5 * first_sum[c]) * (1.0 / 16)
                if e == 0:
                    layers[v - 1, 2 * c] = falling
                    layers[v - 1, 2 * c + 1] = first_sum[c] - falling
                    line = (squares_1[c] - 0.5 * squares_0[c]) * (1.0 / 16)
                    both = (squares_2[c] - squares_1[c]) * (1.0 / 128) + squares_0[c] * (1.0 / 1024)
                    layers[v - 1, 6 + 2 * c] = both
                    layers[v - 1, 6 + 2 * c + 1] = (squares_0[c] - 2.0 * line) + both
                else:
                    layers[v - 1, 2 * c + 1] += falling
                    layers[v - 1, 6 + 2 * c + 1] += squares_0[c]
        return misfit

    lax.fori_loop(1, 3, lambda v, m: slope_group(v, False, m), zeros)
    misfit = lax.fori_loop(3, 7, lambda v, m: slope_group(v, True, m), zeros)
    lax.fori_loop(7, 9, lambda v, m: slope_group(v, False, m), zeros)

    if last:
        leaving = pltpu.make_async_copy(
            residuals.at[pl.ds(lax.axis_index("depth") * 8, 8)], residual_out, refs[9].at[0]
        )
        leaving.start()
    rows_f[...] = jnp.zeros_like(rows_f)
    rows_s[...] = jnp.zeros_like(rows_s)
    rows8 = row_ids((8, 1)).astype(F32)
    for k in range(3):
        sums = [zeros] * 12
        for v in range(1 + 2 * k, 5 + 2 * k):
            weight = 1.0 - jnp.abs((8 * v - HALO - ELEM * k) + 0.5 + rows8) * (1.0 / ELEM)
            square = weight * weight
            if v < 3:
                weight, square = weight * low_flag, square * low_flag
            if v >= 7:
                weight, square = weight * high_flag, square * high_flag
            for n in range(12):
                sums[n] = sums[n] + (weight if n < 6 else square) * layers[v - 1, n]
        for n in range(6):
            at = k * 6 + n
            rows_f[at : at + 1] = jnp.sum(sums[n], axis=0, keepdims=True)
            rows_s[at : at + 1] = jnp.sum(sums[6 + n], axis=0, keepdims=True)
    force = exact_dot(rows_f[...], [over_y[...]]) * (1.0 / 12)
    stiffness = exact_dot(rows_s[...], [over_y2[0], over_y2[1]]) * (1.0 / 144)
    shape24 = (24, LANES)
    rows24 = row_ids(shape24)
    lanes24 = lane_ids(shape24)
    direction = force / (stiffness + LEVENBERG)
    direction = jnp.where(rows24 < 12, direction, direction * high_flag)
    held = jnp.where(lanes24 < 8, direction, 0.0)
    owned = jnp.where(rows24 < 12, held, 0.0)
    descent = jnp.sum(force * owned)
    length = jnp.sum(owned * owned)
    rows_f[...] = exact_dot(held, [along_y[...]])
    curved = zeros
    for v in range(3, 7):
        k = (v - 3) // 2
        share = (8.0 * ((v - 3) % 2) + 0.5 + rows8) * (1.0 / ELEM)
        field = []
        for n in range(6):
            near = rows_f[k * 6 + n : k * 6 + n + 1]
            far = rows_f[k * 6 + 6 + n : k * 6 + 7 + n]
            field.append(near + share * (far - near))
        row = 8 * (v - 3)
        for e in range(2):
            if e == 0:
                move = [field[2 * c] + (field[2 * c + 1] - field[2 * c]) * (1.0 / 32) for c in range(3)]
                gain = [(field[2 * c + 1] - field[2 * c]) * (1.0 / 16) for c in range(3)]
            else:
                move = [field[2 * c + 1] for c in range(3)]
            for j in range(16):
                three = [slopes[c, 16 * e + j, row : row + 8] for c in range(3)]
                projected = (three[0] * move[0] + three[1] * move[1]) + three[2] * move[2]
                projected = projected * projected
                if e == 1:
                    projected = projected * (1.0 - (j + 0.5) / 16.0) ** 2
                curved = curved + projected
                if e == 0 and j < 15:
                    move = [m + g for m, g in zip(move, gain)]
    curvature = jnp.sum(curved) * (1.0 / 144)
    misfit = jnp.sum(misfit)
    line = jnp.sum(jnp.where(pick, direction[0:16], 0.0), axis=0, keepdims=True)
    line_lanes = lane_ids((1, LANES))
    for at, value in ((96, descent), (97, length), (98, curvature), (99, misfit)):
        line = jnp.where(line_lanes == at, value, line)
    block_out[...] = jnp.broadcast_to(line, (tiles, LANES))
    if last:
        leaving.wait()


def iteration(tiles, first, last, motion, received, target, cors, tables):
    vmem = pl.BlockSpec(memory_space=pltpu.VMEM)
    args = [motion] + ([] if first else [received]) + [*target, *cors, *tables]
    shapes = [
        jax.ShapeDtypeStruct((tiles, LANES), F32),
        jax.ShapeDtypeStruct((8, LANES), F32),
    ]
    scratch = [
        pltpu.VMEM((64, LANES), F32),
        pltpu.VMEM((GROUPS, 6, 8, LANES), F32),
        pltpu.VMEM((SLAB + 4, FRAME, LANES), F32),
        pltpu.VMEM((3, SLAB, ROWS, LANES), F32),
        pltpu.VMEM((8, 12, 8, LANES), F32),
        pltpu.VMEM((24, LANES), F32),
        pltpu.VMEM((24, LANES), F32),
        pltpu.VMEM((tiles + 24, LANES), F32),
    ]
    if first:
        shapes.append(jax.ShapeDtypeStruct((SLAB, ROWS + 2 * ELEM, LANES), F32))
    if last:
        shapes.append(jax.ShapeDtypeStruct((8, ROWS, LANES), F32))
        scratch.append(pltpu.VMEM((SLAB, ROWS, LANES), F32))
        scratch.append(pltpu.SemaphoreType.DMA((1,)))
    out_specs = [vmem] * len(shapes)
    if last:
        out_specs[-1] = pl.BlockSpec(memory_space=pltpu.HBM)
    return pl.pallas_call(
        functools.partial(iteration_body, tiles, first, last),
        out_shape=shapes,
        in_specs=[vmem] * len(args),
        out_specs=out_specs,
        scratch_shapes=scratch,
        cost_estimate=pl.CostEstimate(flops=20000000, bytes_accessed=9000000, transcendentals=0),
        name="iteration",
        compiler_params=pltpu.CompilerParams(vmem_limit_bytes=16 * 2**20),
    )(*args)


def finish_body(tiles, motion, got_1, got_2, got_3, chooser, displacement, misfits, padded):
    now = updated_motion(motion, got_3, lax.axis_index("tile"), tiles, padded)
    shape = (8, LANES)
    component = (lane_ids(shape) // 16) % 3
    mine = jnp.where(component == row_ids(shape), jnp.broadcast_to(now[1:2], shape), 0.0)
    mine = jnp.where(lane_ids(shape) < 96, mine, 0.0)
    placed = lax.dot_general(
        mine, chooser[...], (((1,), (1,)), ((), ())), precision=highest, preferred_element_type=F32
    )
    displacement[...] = placed[0:3]
    for n, got in enumerate((got_1, got_2, got_3)):
        total = jnp.sum(got[...], axis=0, keepdims=True)
        misfits[:, n : n + 1] = total[:, 99:100] * (1.0 / VOXELS)


def finish(tiles, motion, got, chooser):
    vmem = pl.BlockSpec(memory_space=pltpu.VMEM)
    return pl.pallas_call(
        functools.partial(finish_body, tiles),
        out_shape=[jax.ShapeDtypeStruct((3, 32), F32), jax.ShapeDtypeStruct((1, 3), F32)],
        in_specs=[vmem] * 5,
        out_specs=[vmem] * 2,
        scratch_shapes=[pltpu.VMEM((tiles + 24, LANES), F32)],
        name="finish",
        compiler_params=pltpu.CompilerParams(vmem_limit_bytes=2**20),
    )(motion, *got, chooser)


def from_behind(block, axis, distance):
    devices = range(lax.axis_size(axis))
    return lax.ppermute(block, axis, [(i - distance, i) for i in devices if i - distance in devices])


def swap(block, first):
    pairs = [(i, i + 1) for i in range(first, lax.axis_size("tile") - 1, 2)]
    return lax.ppermute(block, "tile", pairs + [(j, i) for i, j in pairs])


def ring(block, distance):
    peers = lax.axis_size("depth")
    return lax.ppermute(block, "depth", [((i + distance) % peers, i) for i in range(peers)])


def local(reference_image, deformed_image, offsets, node_ids, start_motion):
    tiles = lax.axis_size("tile")
    zero = jnp.zeros((), F32)
    both = lax.pad(deformed_image, zero, ((0, 8, 0), (0, 0, 0), (0, 0, 0)))
    both = both + lax.pad(reference_image, zero, ((8, 0, 0), (0, 0, 0), (0, 0, 0)))
    both = [both] + [ring(both, n) for n in (1, 2, 3)]
    lines, chooser, *tables = prepare(offsets, node_ids, start_motion)
    other = ring(lines, 2)
    beyond = from_behind(lines, "tile", -2)
    far, far_target, near, extra = pack(*both, lines, other, beyond)
    far = swap(far, 1)
    near = swap(near, 0)
    far_target = swap(far_target, 1)
    (near_cors,) = corner_images(tiles, False, *both, near, extra)
    far_cors, motion = corner_images(tiles, True, *both, far, near, extra)
    cors = (near_cors, far_cors)
    target = (*both, far_target, near)
    received = None
    got = []
    for number in range(ITERS):
        first, last = number == 0, number == ITERS - 1
        outs = iteration(tiles, first, last, motion, received, target, cors, tables)
        block, motion = outs[:2]
        if first:
            target = (outs[2],)
        received = lax.all_to_all(block, "tile", 0, 0, tiled=True)
        got.append(received)
    displacement, misfits = finish(tiles, motion, got, chooser)
    return displacement, misfits.reshape(3), outs[2]


def solution(mesh):
    in_specs = (
        P("depth", "tile", None),
        P("depth", "tile", None),
        P(None, "depth", "tile", None),
        P(None, "tile", None),
        P(None, "tile"),
    )
    out_specs = (P(None, "tile"), P(), P("depth", "tile", None))
    return jax.shard_map(local, mesh=mesh, in_specs=in_specs, out_specs=out_specs, check_vma=False)
```

```python
import functools

import jax
import jax.numpy as jnp
from jax import lax
from jax.experimental import pallas as pl
from jax.experimental.pallas import tpu as pltpu
from jax.sharding import PartitionSpec as P

ELEM = 16
ITERS = 3
SLAB = 32
ROWS = 32
LANES = 128
HALO = 24
REACH = 20
FRAME = ROWS + 2 * HALO
GROUPS = FRAME // 8
LEVENBERG = 0.1 * ELEM**3
VOXELS = 8388608.0
F32 = jnp.float32

highest = lax.Precision.HIGHEST


def dot(left, right):
    return jnp.dot(left, right, precision=highest, preferred_element_type=F32)


def split(value, parts):
    pieces = []
    for _ in range(parts):
        piece = value.astype(jnp.bfloat16)
        pieces.append(piece)
        value = value - piece.astype(F32)
    return pieces


def exact_dot(left, tables):
    left = jnp.concatenate(split(left, 3) * len(tables), axis=1)
    right = jnp.concatenate([table for table in tables for _ in range(3)], axis=0)
    return jnp.dot(left, right, preferred_element_type=F32)


def aligned(row):
    return row if isinstance(row, int) else pl.multiple_of(row, 8)


def lane_ids(shape):
    return lax.broadcasted_iota(jnp.int32, shape, 1)


def row_ids(shape):
    return lax.broadcasted_iota(jnp.int32, shape, 0)


def along_y_table(shape, lane_axis):
    y = lax.broadcasted_iota(jnp.int32, shape, 1 - lane_axis).astype(F32) + 0.5
    places = (lax.broadcasted_iota(jnp.int32, shape, lane_axis) % 8 * ELEM).astype(F32)
    return jnp.maximum(1.0 - jnp.abs(y - places) * (1.0 / ELEM), 0.0)


def prepare_body(offsets, far_ids, far_motion, *refs):
    lines, chooser, along_y, over_y, over_y2 = refs[:5]
    held, node_ids, start_motion, sem = refs[5:]
    nodes = [
        pltpu.make_async_copy(far_ids, node_ids, sem.at[6]),
        pltpu.make_async_copy(far_motion, start_motion, sem.at[7]),
    ]
    picked = [
        pltpu.make_async_copy(
            offsets.at[c, 0, pl.ds(ELEM * ex, 8)], held.at[2 * c + ex], sem.at[2 * c + ex]
        )
        for c in range(3)
        for ex in range(2)
    ]
    for copy in nodes + picked:
        copy.start()
    for copy in nodes:
        copy.wait()
    shape = (8, LANES)
    lanes = lane_ids(shape)
    eight = jnp.where(lanes % 8 == row_ids(shape), 1.0, 0.0)
    ids = jnp.zeros((1, LANES), F32)
    lanes1 = lane_ids((1, LANES))
    group = lanes1 // 8
    for k in range(2):
        for a in range(2):
            wide = dot((node_ids[a, k : k + 1] % 32).astype(F32), eight)
            ids = jnp.where((group // 6 == k) & (group % 2 == a), wide, ids)
    ids = jnp.where(lanes1 < 96, ids, -1.0)
    chosen = jnp.where(row_ids((32, LANES)).astype(F32) == ids, 1.0, 0.0)
    chooser[...] = chosen
    taken = dot(start_motion[...], chosen)
    component = (lane_ids((3, LANES)) // 16) % 3
    line = jnp.sum(
        jnp.where(component == row_ids((3, LANES)), taken, 0.0), axis=0, keepdims=True
    )
    square = (LANES, LANES)
    along_y[...] = along_y_table(square, 0).astype(jnp.bfloat16)
    table = along_y_table(square, 1)
    over_y[...] = table.astype(jnp.bfloat16)
    over_y2[0], over_y2[1] = split(table * table, 2)
    lines[...] = jnp.broadcast_to(line, shape)
    for n, copy in enumerate(picked):
        copy.wait()
        lines[n : n + 1] = held[n, 0:1].astype(F32)


def prepare(offsets, node_ids, start_motion):
    vmem = pl.BlockSpec(memory_space=pltpu.VMEM)
    outside = pl.BlockSpec(memory_space=pltpu.HBM)
    shapes = [jax.ShapeDtypeStruct((n, LANES), F32) for n in (8, 32)]
    for size in ((LANES, LANES), (LANES, LANES), (2, LANES, LANES)):
        shapes.append(jax.ShapeDtypeStruct(size, jnp.bfloat16))
    return pl.pallas_call(
        prepare_body,
        out_shape=shapes,
        in_specs=[outside] * 3,
        out_specs=[vmem] * len(shapes),
        scratch_shapes=[
            pltpu.VMEM((6, 8, LANES), jnp.int32),
            pltpu.VMEM(node_ids.shape, jnp.int32),
            pltpu.VMEM(start_motion.shape, F32),
            pltpu.SemaphoreType.DMA((8,)),
        ],
        name="prepare",
        compiler_params=pltpu.CompilerParams(vmem_limit_bytes=2 * 2**20),
    )(offsets, node_ids, start_motion)


def pack_body(*refs):
    both = refs[:4]
    lines, other, beyond, far, far_target, near, extra = refs[4:]
    depth = lax.axis_index("depth")
    odd = lax.rem(lax.axis_index("tile"), 2)
    far_rows = pl.ds((ROWS - REACH) * odd, REACH)
    near_rows = pl.ds(pl.multiple_of(8 * (1 - odd), 8), HALO)
    for step, piece in enumerate(both):
        planes = pl.ds(lax.rem(depth + step, 4) * 8, 8)
        for n in range(8):
            to = pl.ds((lax.rem(depth + step, 4) * 8 + n) * REACH, REACH)
            far[to] = piece[n, far_rows]
        near[planes, :HALO] = piece[0:8, near_rows]
        far_target[planes] = piece[8:16, pl.ds(pl.multiple_of(ELEM * odd, 8), ELEM)]
        near[planes, HALO:] = piece[8:16, pl.ds(pl.multiple_of(ELEM * (1 - odd), 8), ELEM)]
    upper = depth >= 2
    mine, given = lines[0:6], other[0:6]
    extra[...] = jnp.zeros_like(extra)
    extra[0:6] = jnp.where(upper, given, mine)
    extra[6:12] = jnp.where(upper, mine, given)
    extra[12:13] = lines[6:7]
    extra[13:14] = beyond[6:7]
    far[SLAB * REACH :] = extra[0:16]
    near[SLAB, :HALO] = extra[...]
    near[SLAB, HALO:] = jnp.zeros((ELEM, LANES), F32)


def pack(*args):
    shapes = (
        (SLAB * REACH + 16, LANES),
        (SLAB, ELEM, LANES),
        (SLAB + 1, HALO + ELEM, LANES),
        (HALO, LANES),
    )
    vmem = pl.BlockSpec(memory_space=pltpu.VMEM)
    return pl.pallas_call(
        pack_body,
        out_shape=[jax.ShapeDtypeStruct(shape, F32) for shape in shapes],
        in_specs=[vmem] * len(args),
        out_specs=[vmem] * len(shapes),
        cost_estimate=pl.CostEstimate(flops=0, bytes_accessed=2000000, transcendentals=0),
        name="pack",
        compiler_params=pltpu.CompilerParams(vmem_limit_bytes=4 * 2**20),
    )(*args)


def near_base(odd):
    return 4 * (1 - odd)


def far_base(odd):
    return 6 * odd


def corner_body(tiles, is_far, own, one, two, three, part, *refs):
    if is_far:
        near, extra, chunk, motion, source, shifted, table = refs
    else:
        extra, chunk, source, shifted, table = refs
    tile = lax.axis_index("tile")
    depth = lax.axis_index("depth")
    odd = lax.rem(tile, 2)
    if is_far:
        motion[...] = jnp.zeros_like(motion)
        motion[1:2] = extra[12:13]
        motion[3:4] = extra[13:14]
        motion[pl.ds(2 * odd, 1)] = part[SLAB * REACH + 12 : SLAB * REACH + 13]
        motion[pl.ds(2 - 2 * odd, 1)] = near[SLAB, 12:13]
    right = odd if is_far else 1 - odd
    base = far_base(odd) if is_far else near_base(odd)
    if is_far:
        rows = pl.ds(8 + HALO - REACH + (ROWS + REACH) * right, REACH)
        for z in range(SLAB):
            source[z, rows] = part[z * REACH : (z + 1) * REACH]
    else:
        rows = pl.ds(pl.multiple_of(8 + (HALO + ROWS) * right, 8), HALO)
        source[:, rows] = part[0:SLAB, :HALO]
    for step, piece in enumerate((own, one, two, three)):
        start = lax.rem(depth + step, 4) * 8
        source[pl.ds(start, 8), 8 + HALO : 8 + HALO + ROWS] = piece[0:8]
    for e in range(2):
        for c in range(3):
            for which in range(2):
                at = e * 6 + c * 2 + which
                row = (e * 6 + which) * 3 + c
                table[row + 6 : row + 7] = extra[at : at + 1]
                if is_far:
                    line = part[SLAB * REACH + at : SLAB * REACH + at + 1]
                else:
                    line = part[SLAB, at : at + 1]
                table[pl.ds(row + 12 * right, 1)] = line

    shape = (8, LANES)
    lanes = lane_ids(shape)
    zeros = jnp.zeros(shape, F32)

    def group(number, carry):
        v = base + number
        ex = (v + 1) // 2
        outside = ((tile == 0) & (v < 3)) | ((tile == tiles - 1) & (v >= 7))
        inside = jnp.where(outside, 0.0, 1.0).astype(F32)
        for e in range(2):
            offs = [
                jnp.broadcast_to(table[pl.ds((e * 6 + ex) * 3 + c, 1)], shape) for c in range(3)
            ]
            reach = lanes + offs[2].astype(jnp.int32)
            picks = []
            for s in range(2):
                at = reach + s
                good = jnp.where((at >= 0) & (at < LANES), inside, 0.0)
                picks.append((jnp.clip(at, 0, LANES - 1), good))
            is_x = [offs[1] == float(o) for o in (-2, -1, 0)]
            odd_z = (offs[0] == -1.0) | (offs[0] == 1.0)
            high_z = offs[0] >= 0.0
            planes = []
            steps = []
            for p in range(20):
                z = 16 * e + p - 2
                corners = [zeros] * 4
                if 0 <= z < SLAB:
                    for half in range(2):
                        block = source[z, pl.ds(8 * v + 6 + 4 * half, 8)]
                        for s in range(2):
                            index, good = picks[s]
                            taken = jnp.take_along_axis(
                                block, index, axis=1, mode="promise_in_bounds"
                            )
                            shifted[e, s, p, 4 * half : 4 * half + 8] = taken * good
                    corners = []
                    for sx in range(2):
                        for sy in range(2):
                            rows = [shifted[e, sy, p, sx + o : sx + o + 8] for o in range(4)]
                            corners.append(
                                jnp.where(
                                    is_x[0],
                                    rows[0],
                                    jnp.where(
                                        is_x[1], rows[1], jnp.where(is_x[2], rows[2], rows[3])
                                    ),
                                )
                            )
                planes.append(corners)
                if p >= 1:
                    steps.append(
                        [jnp.where(odd_z, planes[p][n], planes[p - 1][n]) for n in range(4)]
                    )
                if p >= 3:
                    c00, c01, c10, c11 = [
                        jnp.where(high_z, steps[p - 1][n], steps[p - 3][n]) for n in range(4)
                    ]
                    along = c01 - c00
                    chunk[number, e, p - 3, 0] = c00
                    chunk[number, e, p - 3, 1] = along
                    chunk[number, e, p - 3, 2] = c10 - c00
                    chunk[number, e, p - 3, 3] = (c11 - c10) - along
        return carry

    lax.fori_loop(0, chunk.shape[0], group, 0)


def corner_images(tiles, is_far, *args):
    vmem = pl.BlockSpec(memory_space=pltpu.VMEM)
    shapes = [(4 if is_far else 6, 2, 17, 4, 8, LANES)] + ([(8, LANES)] if is_far else [])
    return pl.pallas_call(
        functools.partial(corner_body, tiles, is_far),
        out_shape=[jax.ShapeDtypeStruct(shape, F32) for shape in shapes],
        in_specs=[vmem] * len(args),
        out_specs=[vmem] * len(shapes),
        scratch_shapes=[
            pltpu.VMEM((SLAB, FRAME + 16, LANES), F32),
            pltpu.VMEM((2, 2, 20, 16, LANES), F32),
            pltpu.VMEM((40, LANES), F32),
        ],
        cost_estimate=pl.CostEstimate(flops=5000000, bytes_accessed=4000000, transcendentals=0),
        name="corners_far" if is_far else "corners_near",
        compiler_params=pltpu.CompilerParams(vmem_limit_bytes=8 * 2**20),
    )(*args)


def updated_motion(motion, received, tile, tiles, padded):
    padded[...] = jnp.zeros_like(padded)
    padded[8 : 8 + tiles] = received[...]
    total = jnp.sum(received[...], axis=0, keepdims=True)
    descent = total[:, 96:97]
    length = total[:, 97:98]
    curvature = total[:, 98:99]
    step = descent / (curvature + LEVENBERG * length)
    near = padded[pl.ds(7 + tile, 8)]
    return motion[...] - step * near


def own_lanes():
    shape = (16, LANES)
    return (lane_ids(shape) // 8 == row_ids(shape)) & (row_ids(shape) < 12)


def warp_image(now, odd, near_cors, far_cors, along_y, wide, ends, warped):
    shape16 = (16, LANES)
    pick = own_lanes()
    spread = jnp.concatenate(
        [jnp.where(pick, jnp.broadcast_to(now[n : n + 1], shape16), 0.0) for n in range(4)], axis=0
    )
    wide[...] = exact_dot(spread, [along_y[...]])

    zero = jnp.zeros((2, FRAME, LANES), F32)
    warped[0:2] = zero
    warped[SLAB + 2 : SLAB + 4] = zero

    shares = (row_ids((8, LANES)).astype(F32) + 0.5) * (1.0 / ELEM)
    for v in range(GROUPS):
        node = (v + 1) // 2
        lower = 16 * (node // 2) + 6 * (node % 2)
        upper = 16 * ((node + 1) // 2) + 6 * ((node + 1) % 2)
        share = shares + 0.5 * ((v + 1) % 2)
        for n in range(6):
            begin = wide[lower + n : lower + n + 1]
            ends[v, n] = begin + share * (wide[upper + n : upper + n + 1] - begin)

    def warp(cors, base, number, carry):
        v = base + number
        at = pl.ds(pl.multiple_of(8 * v, 8), 8)
        near = [ends[v, 2 * c] for c in range(3)]
        far = [ends[v, 2 * c + 1] for c in range(3)]
        for e in range(2):
            if e == 0:
                move = [n + (f - n) * (1.0 / 32) for n, f in zip(near, far)]
                gain = [(f - n) * (1.0 / 16) for n, f in zip(near, far)]
            else:
                move = [f * (31.0 / 32) for f in far]
                gain = [f * (-1.0 / 16) for f in far]
            plane = [cors[number, e, 0, n] for n in range(4)]
            for j in range(16):
                above = [cors[number, e, j + 1, n] for n in range(4)]
                mz, mx, my = move
                here = (plane[0] + my * plane[1]) + mx * (plane[2] + my * plane[3])
                there = (above[0] + my * above[1]) + mx * (above[2] + my * above[3])
                warped[2 + 16 * e + j, at] = here + mz * (there - here)
                plane = above
                if j < 15:
                    move = [m + g for m, g in zip(move, gain)]
        return carry

    lax.fori_loop(0, 6, functools.partial(warp, near_cors, near_base(odd)), 0)
    lax.fori_loop(0, 4, functools.partial(warp, far_cors, far_base(odd)), 0)


def warp_body(motion, near_cors, far_cors, along_y, warped, wide, ends):
    odd = lax.rem(lax.axis_index("tile"), 2)
    warp_image(motion[...], odd, near_cors, far_cors, along_y, wide, ends, warped)


def first_warp(motion, cors, along_y):
    vmem = pl.BlockSpec(memory_space=pltpu.VMEM)
    return pl.pallas_call(
        warp_body,
        out_shape=jax.ShapeDtypeStruct((SLAB + 4, FRAME, LANES), F32),
        in_specs=[vmem] * 4,
        out_specs=vmem,
        scratch_shapes=[
            pltpu.VMEM((64, LANES), F32),
            pltpu.VMEM((GROUPS, 6, 8, LANES), F32),
        ],
        cost_estimate=pl.CostEstimate(flops=4000000, bytes_accessed=7000000, transcendentals=0),
        name="warp",
        compiler_params=pltpu.CompilerParams(vmem_limit_bytes=4 * 2**20),
    )(motion, *cors, along_y)


def iteration_body(tiles, first, last, *refs):
    refs = list(refs)
    motion = refs.pop(0)
    received = None if first else refs.pop(0)
    if first:
        pieces, refs = refs[:6], refs[6:]
    else:
        target = refs.pop(0)
    if first:
        warped = refs.pop(0)
    else:
        near_cors, far_cors, refs = refs[0], refs[1], refs[2:]
    along_y, over_y, over_y2, block_out, motion_out = refs[:5]
    refs = refs[5:]
    if first:
        target = refs.pop(0)
    residual_out = refs.pop(0) if last else None
    slopes, layers, rows_f, rows_s, padded = refs[:5]
    if not first:
        wide, ends, warped = refs[5:8]
    residuals = refs[8] if last else None

    tile = lax.axis_index("tile")
    odd = lax.rem(tile, 2)
    if first:
        depth = lax.axis_index("depth")
        for step, piece in enumerate(pieces[:4]):
            start = lax.rem(depth + step, 4) * 8
            target[pl.ds(start, 8), ELEM : ELEM + ROWS] = piece[8:16]
        far = pl.ds(pl.multiple_of((ELEM + ROWS) * odd, 8), ELEM)
        near = pl.ds(pl.multiple_of((ELEM + ROWS) * (1 - odd), 8), ELEM)
        target[:, far] = pieces[4][...]
        target[:, near] = pieces[5][0:SLAB, HALO:]
    low_flag = jnp.where(tile > 0, 1.0, 0.0).astype(F32)
    high_flag = jnp.where(tile < tiles - 1, 1.0, 0.0).astype(F32)
    now = motion[...] if first else updated_motion(motion, received, tile, tiles, padded)
    motion_out[...] = now
    if not first:
        warp_image(now, odd, near_cors, far_cors, along_y, wide, ends, warped)

    shape = (8, LANES)
    lanes = lane_ids(shape)
    ahead_1 = jnp.where(lanes < LANES - 1, 8.0, 0.0)
    behind_1 = jnp.where(lanes > 0, 8.0, 0.0)
    ahead_2 = jnp.where(lanes < LANES - 2, 1.0, 0.0)
    behind_2 = jnp.where(lanes > 1, 1.0, 0.0)
    zeros = jnp.zeros(shape, F32)

    def slope_group(v, own, misfit):
        at = pl.ds(aligned(8 * v), 8)
        row = aligned(8 * (v - 3))
        goal = pl.ds(aligned(8 * (v - 1)), 8)
        planes = [warped[n, at] for n in range(4)]
        for e in range(2):
            first_sum = [zeros] * 3
            second_sum = [zeros] * 3
            squares_0 = [zeros] * 3
            squares_1 = [zeros] * 3
            squares_2 = [zeros] * 3
            for j in range(16):
                z = 16 * e + j
                planes.append(warped[z + 4, at])
                mid = planes[2]
                slope_z = 8.0 * (planes[3] - planes[1]) - (planes[4] - planes[0])
                planes = planes[1:]
                up_1 = warped[z + 2, pl.ds(8 * v + 1, 8)]
                up_2 = warped[z + 2, pl.ds(8 * v + 2, 8)]
                down_1 = warped[z + 2, pl.ds(8 * v - 1, 8)]
                down_2 = warped[z + 2, pl.ds(8 * v - 2, 8)]
                slope_x = 8.0 * (up_1 - down_1) - (up_2 - down_2)
                slope_y = (
                    ahead_1 * pltpu.roll(mid, LANES - 1, 1) - behind_1 * pltpu.roll(mid, 1, 1)
                ) - (ahead_2 * pltpu.roll(mid, LANES - 2, 1) - behind_2 * pltpu.roll(mid, 2, 1))
                residual = mid - target[z, goal]
                three = (slope_z, slope_x, slope_y)
                if own:
                    misfit = misfit + residual * residual
                    for c in range(3):
                        slopes[c, z, pl.ds(row, 8)] = three[c]
                    if last:
                        residuals[z, pl.ds(row, 8)] = residual
                weight = 1.0 - (j + 0.5) / 16.0
                for c in range(3):
                    first_sum[c] = first_sum[c] + three[c] * residual
                    second_sum[c] = second_sum[c] + first_sum[c]
                    square = three[c] * three[c]
                    if e == 0:
                        squares_0[c] = squares_0[c] + square
                        squares_1[c] = squares_1[c] + squares_0[c]
                        squares_2[c] = squares_2[c] + squares_1[c]
                    else:
                        squares_0[c] = squares_0[c] + (weight * weight) * square
            for c in range(3):
                falling = (second_sum[c] - 0.5 * first_sum[c]) * (1.0 / 16)
                if e == 0:
                    layers[v - 1, 2 * c] = falling
                    layers[v - 1, 2 * c + 1] = first_sum[c] - falling
                    line = (squares_1[c] - 0.5 * squares_0[c]) * (1.0 / 16)
                    both = (squares_2[c] - squares_1[c]) * (1.0 / 128) + squares_0[c] * (1.0 / 1024)
                    layers[v - 1, 6 + 2 * c] = both
                    layers[v - 1, 6 + 2 * c + 1] = (squares_0[c] - 2.0 * line) + both
                else:
                    layers[v - 1, 2 * c + 1] += falling
                    layers[v - 1, 6 + 2 * c + 1] += squares_0[c]
        return misfit

    def two_groups(number, misfit):
        misfit = slope_group(3 + 2 * number, True, misfit)
        return slope_group(4 + 2 * number, True, misfit)

    slope_group(1, False, zeros)
    slope_group(2, False, zeros)
    misfit = lax.fori_loop(0, 2, two_groups, zeros)
    slope_group(7, False, zeros)
    slope_group(8, False, zeros)

    if last:
        leaving = pltpu.make_async_copy(
            residuals.at[pl.ds(lax.axis_index("depth") * 8, 8)], residual_out, refs[9].at[0]
        )
        leaving.start()
    rows_f[...] = jnp.zeros_like(rows_f)
    rows_s[...] = jnp.zeros_like(rows_s)
    rows8 = row_ids((8, 1)).astype(F32)
    for k in range(3):
        sums = [zeros] * 12
        for v in range(1 + 2 * k, 5 + 2 * k):
            weight = 1.0 - jnp.abs((8 * v - HALO - ELEM * k) + 0.5 + rows8) * (1.0 / ELEM)
            square = weight * weight
            if v < 3:
                weight, square = weight * low_flag, square * low_flag
            if v >= 7:
                weight, square = weight * high_flag, square * high_flag
            for n in range(12):
                sums[n] = sums[n] + (weight if n < 6 else square) * layers[v - 1, n]
        for n in range(6):
            at = k * 6 + n
            rows_f[at : at + 1] = jnp.sum(sums[n], axis=0, keepdims=True)
            rows_s[at : at + 1] = jnp.sum(sums[6 + n], axis=0, keepdims=True)
    force = exact_dot(rows_f[...], [over_y[...]]) * (1.0 / 12)
    stiffness = exact_dot(rows_s[...], [over_y2[0], over_y2[1]]) * (1.0 / 144)
    shape24 = (24, LANES)
    rows24 = row_ids(shape24)
    lanes24 = lane_ids(shape24)
    direction = force / (stiffness + LEVENBERG)
    direction = jnp.where(rows24 < 12, direction, direction * high_flag)
    held = jnp.where(lanes24 < 8, direction, 0.0)
    owned = jnp.where(rows24 < 12, held, 0.0)
    descent = jnp.sum(force * owned)
    length = jnp.sum(owned * owned)
    rows_f[...] = exact_dot(held, [along_y[...]])
    curved = zeros
    for v in range(3, 7):
        k = (v - 3) // 2
        share = (8.0 * ((v - 3) % 2) + 0.5 + rows8) * (1.0 / ELEM)
        field = []
        for n in range(6):
            near = rows_f[k * 6 + n : k * 6 + n + 1]
            far = rows_f[k * 6 + 6 + n : k * 6 + 7 + n]
            field.append(near + share * (far - near))
        row = 8 * (v - 3)
        for e in range(2):
            if e == 0:
                move = [field[2 * c] + (field[2 * c + 1] - field[2 * c]) * (1.0 / 32) for c in range(3)]
                gain = [(field[2 * c + 1] - field[2 * c]) * (1.0 / 16) for c in range(3)]
            else:
                move = [field[2 * c + 1] for c in range(3)]
            for j in range(16):
                three = [slopes[c, 16 * e + j, row : row + 8] for c in range(3)]
                projected = (three[0] * move[0] + three[1] * move[1]) + three[2] * move[2]
                projected = projected * projected
                if e == 1:
                    projected = projected * (1.0 - (j + 0.5) / 16.0) ** 2
                curved = curved + projected
                if e == 0 and j < 15:
                    move = [m + g for m, g in zip(move, gain)]
    curvature = jnp.sum(curved) * (1.0 / 144)
    misfit = jnp.sum(misfit)
    line = jnp.sum(jnp.where(own_lanes(), direction[0:16], 0.0), axis=0, keepdims=True)
    line_lanes = lane_ids((1, LANES))
    for at, value in ((96, descent), (97, length), (98, curvature), (99, misfit)):
        line = jnp.where(line_lanes == at, value, line)
    block_out[...] = jnp.broadcast_to(line, (tiles, LANES))
    if last:
        leaving.wait()


def iteration(tiles, first, last, motion, received, target, cors, tables):
    vmem = pl.BlockSpec(memory_space=pltpu.VMEM)
    args = [motion] + ([] if first else [received]) + [*target, *cors, *tables]
    shapes = [
        jax.ShapeDtypeStruct((tiles, LANES), F32),
        jax.ShapeDtypeStruct((8, LANES), F32),
    ]
    scratch = [
        pltpu.VMEM((3, SLAB, ROWS, LANES), F32),
        pltpu.VMEM((8, 12, 8, LANES), F32),
        pltpu.VMEM((24, LANES), F32),
        pltpu.VMEM((24, LANES), F32),
        pltpu.VMEM((tiles + 24, LANES), F32),
    ]
    if not first:
        scratch += [
            pltpu.VMEM((64, LANES), F32),
            pltpu.VMEM((GROUPS, 6, 8, LANES), F32),
            pltpu.VMEM((SLAB + 4, FRAME, LANES), F32),
        ]
    if first:
        shapes.append(jax.ShapeDtypeStruct((SLAB, ROWS + 2 * ELEM, LANES), F32))
    if last:
        shapes.append(jax.ShapeDtypeStruct((8, ROWS, LANES), F32))
        scratch.append(pltpu.VMEM((SLAB, ROWS, LANES), F32))
        scratch.append(pltpu.SemaphoreType.DMA((1,)))
    out_specs = [vmem] * len(shapes)
    if last:
        out_specs[-1] = pl.BlockSpec(memory_space=pltpu.HBM)
    return pl.pallas_call(
        functools.partial(iteration_body, tiles, first, last),
        out_shape=shapes,
        in_specs=[vmem] * len(args),
        out_specs=out_specs,
        scratch_shapes=scratch,
        cost_estimate=pl.CostEstimate(flops=20000000, bytes_accessed=9000000, transcendentals=0),
        name="iteration",
        compiler_params=pltpu.CompilerParams(vmem_limit_bytes=16 * 2**20),
    )(*args)


def finish_body(tiles, motion, got_1, got_2, got_3, chooser, displacement, misfits, padded):
    now = updated_motion(motion, got_3, lax.axis_index("tile"), tiles, padded)
    shape = (8, LANES)
    component = (lane_ids(shape) // 16) % 3
    mine = jnp.where(component == row_ids(shape), jnp.broadcast_to(now[1:2], shape), 0.0)
    mine = jnp.where(lane_ids(shape) < 96, mine, 0.0)
    placed = lax.dot_general(
        mine, chooser[...], (((1,), (1,)), ((), ())), precision=highest, preferred_element_type=F32
    )
    displacement[...] = placed[0:3]
    for n, got in enumerate((got_1, got_2, got_3)):
        total = jnp.sum(got[...], axis=0, keepdims=True)
        misfits[:, n : n + 1] = total[:, 99:100] * (1.0 / VOXELS)


def finish(tiles, motion, got, chooser):
    vmem = pl.BlockSpec(memory_space=pltpu.VMEM)
    return pl.pallas_call(
        functools.partial(finish_body, tiles),
        out_shape=[jax.ShapeDtypeStruct((3, 32), F32), jax.ShapeDtypeStruct((1, 3), F32)],
        in_specs=[vmem] * 5,
        out_specs=[vmem] * 2,
        scratch_shapes=[pltpu.VMEM((tiles + 24, LANES), F32)],
        name="finish",
        compiler_params=pltpu.CompilerParams(vmem_limit_bytes=2**20),
    )(motion, *got, chooser)


def from_behind(block, axis, distance):
    devices = range(lax.axis_size(axis))
    return lax.ppermute(block, axis, [(i - distance, i) for i in devices if i - distance in devices])


def swap(block, first):
    pairs = [(i, i + 1) for i in range(first, lax.axis_size("tile") - 1, 2)]
    return lax.ppermute(block, "tile", pairs + [(j, i) for i, j in pairs])


def ring(block, distance):
    peers = lax.axis_size("depth")
    return lax.ppermute(block, "depth", [((i + distance) % peers, i) for i in range(peers)])


def local(reference_image, deformed_image, offsets, node_ids, start_motion):
    tiles = lax.axis_size("tile")
    zero = jnp.zeros((), F32)
    both = lax.pad(deformed_image, zero, ((0, 8, 0), (0, 0, 0), (0, 0, 0)))
    both = both + lax.pad(reference_image, zero, ((8, 0, 0), (0, 0, 0), (0, 0, 0)))
    both = [both] + [ring(both, n) for n in (1, 2, 3)]
    lines, chooser, *tables = prepare(offsets, node_ids, start_motion)
    other = ring(lines, 2)
    beyond = from_behind(lines, "tile", -2)
    far, far_target, near, extra = pack(*both, lines, other, beyond)
    far = swap(far, 1)
    near = swap(near, 0)
    far_target = swap(far_target, 1)
    (near_cors,) = corner_images(tiles, False, *both, near, extra)
    far_cors, motion = corner_images(tiles, True, *both, far, near, extra)
    cors = (near_cors, far_cors)
    warped = first_warp(motion, cors, tables[0])
    target = (*both, far_target, near)
    received = None
    got = []
    for number in range(ITERS):
        first, last = number == 0, number == ITERS - 1
        sources = (warped,) if first else cors
        outs = iteration(tiles, first, last, motion, received, target, sources, tables)
        block, motion = outs[:2]
        if first:
            target = (outs[2],)
        received = lax.all_to_all(block, "tile", 0, 0, tiled=True)
        got.append(received)
    displacement, misfits = finish(tiles, motion, got, chooser)
    return displacement, misfits.reshape(3), outs[2]


def solution(mesh):
    in_specs = (
        P("depth", "tile", None),
        P("depth", "tile", None),
        P(None, "depth", "tile", None),
        P(None, "tile", None),
        P(None, "tile"),
    )
    out_specs = (P(None, "tile"), P(), P("depth", "tile", None))
    return jax.shard_map(local, mesh=mesh, in_specs=in_specs, out_specs=out_specs, check_vma=False)
```

```python
import functools

import jax
import jax.numpy as jnp
from jax import lax
from jax.experimental import pallas as pl
from jax.experimental.pallas import tpu as pltpu
from jax.sharding import PartitionSpec as P

ELEM = 16
ITERS = 3
SLAB = 32
ROWS = 32
LANES = 128
HALO = 24
REACH = 20
FRAME = ROWS + 2 * HALO
GROUPS = FRAME // 8
LEVENBERG = 0.1 * ELEM**3
VOXELS = 8388608.0
F32 = jnp.float32

highest = lax.Precision.HIGHEST


def dot(left, right):
    return jnp.dot(left, right, precision=highest, preferred_element_type=F32)


def split(value, parts):
    pieces = []
    for _ in range(parts):
        piece = value.astype(jnp.bfloat16)
        pieces.append(piece)
        value = value - piece.astype(F32)
    return pieces


def exact_dot(left, tables):
    left = jnp.concatenate(split(left, 3) * len(tables), axis=1)
    right = jnp.concatenate([table for table in tables for _ in range(3)], axis=0)
    return jnp.dot(left, right, preferred_element_type=F32)


def aligned(row):
    return row if isinstance(row, int) else pl.multiple_of(row, 8)


def lane_ids(shape):
    return lax.broadcasted_iota(jnp.int32, shape, 1)


def row_ids(shape):
    return lax.broadcasted_iota(jnp.int32, shape, 0)


def along_y_table(shape, lane_axis):
    y = lax.broadcasted_iota(jnp.int32, shape, 1 - lane_axis).astype(F32) + 0.5
    places = (lax.broadcasted_iota(jnp.int32, shape, lane_axis) % 8 * ELEM).astype(F32)
    return jnp.maximum(1.0 - jnp.abs(y - places) * (1.0 / ELEM), 0.0)


def prepare_body(offsets, far_ids, far_motion, *refs):
    lines, chooser, along_y, over_y, over_y2 = refs[:5]
    held, node_ids, start_motion, sem = refs[5:]
    nodes = [
        pltpu.make_async_copy(far_ids, node_ids, sem.at[6]),
        pltpu.make_async_copy(far_motion, start_motion, sem.at[7]),
    ]
    picked = [
        pltpu.make_async_copy(
            offsets.at[c, 0, pl.ds(ELEM * ex, 8)], held.at[2 * c + ex], sem.at[2 * c + ex]
        )
        for c in range(3)
        for ex in range(2)
    ]
    for copy in nodes + picked:
        copy.start()
    for copy in nodes:
        copy.wait()
    shape = (8, LANES)
    lanes = lane_ids(shape)
    eight = jnp.where(lanes % 8 == row_ids(shape), 1.0, 0.0)
    ids = jnp.zeros((1, LANES), F32)
    lanes1 = lane_ids((1, LANES))
    group = lanes1 // 8
    for k in range(2):
        for a in range(2):
            wide = dot((node_ids[a, k : k + 1] % 32).astype(F32), eight)
            ids = jnp.where((group // 6 == k) & (group % 2 == a), wide, ids)
    ids = jnp.where(lanes1 < 96, ids, -1.0)
    chosen = jnp.where(row_ids((32, LANES)).astype(F32) == ids, 1.0, 0.0)
    wide = jnp.where(row_ids((LANES, LANES)).astype(F32) == ids, 1.0, 0.0)
    chooser[...] = wide.T.astype(jnp.bfloat16)
    taken = dot(start_motion[...], chosen)
    component = (lane_ids((3, LANES)) // 16) % 3
    line = jnp.sum(
        jnp.where(component == row_ids((3, LANES)), taken, 0.0), axis=0, keepdims=True
    )
    square = (LANES, LANES)
    along_y[...] = along_y_table(square, 0).astype(jnp.bfloat16)
    table = along_y_table(square, 1)
    over_y[...] = table.astype(jnp.bfloat16)
    over_y2[0], over_y2[1] = split(table * table, 2)
    lines[...] = jnp.broadcast_to(line, shape)
    for n, copy in enumerate(picked):
        copy.wait()
        lines[n : n + 1] = held[n, 0:1].astype(F32)


def prepare(offsets, node_ids, start_motion):
    vmem = pl.BlockSpec(memory_space=pltpu.VMEM)
    outside = pl.BlockSpec(memory_space=pltpu.HBM)
    shapes = [jax.ShapeDtypeStruct((8, LANES), F32)]
    for size in ((LANES, LANES),) * 3 + ((2, LANES, LANES),):
        shapes.append(jax.ShapeDtypeStruct(size, jnp.bfloat16))
    return pl.pallas_call(
        prepare_body,
        out_shape=shapes,
        in_specs=[outside] * 3,
        out_specs=[vmem] * len(shapes),
        scratch_shapes=[
            pltpu.VMEM((6, 8, LANES), jnp.int32),
            pltpu.VMEM(node_ids.shape, jnp.int32),
            pltpu.VMEM(start_motion.shape, F32),
            pltpu.SemaphoreType.DMA((8,)),
        ],
        name="prepare",
        compiler_params=pltpu.CompilerParams(vmem_limit_bytes=2 * 2**20),
    )(offsets, node_ids, start_motion)


def pack_body(*refs):
    both = refs[:4]
    lines, other, beyond, far, far_target, near, extra = refs[4:]
    depth = lax.axis_index("depth")
    odd = lax.rem(lax.axis_index("tile"), 2)
    far_rows = pl.ds((ROWS - REACH) * odd, REACH)
    near_rows = pl.ds((ROWS - REACH) * (1 - odd), REACH)
    for step, piece in enumerate(both):
        planes = pl.ds(lax.rem(depth + step, 4) * 8, 8)
        for n in range(8):
            to = pl.ds((lax.rem(depth + step, 4) * 8 + n) * REACH, REACH)
            far[to] = piece[n, far_rows]
            near[to] = piece[n, near_rows]
        far_target[planes] = piece[8:16, pl.ds(pl.multiple_of(ELEM * odd, 8), ELEM)]
    upper = depth >= 2
    mine, given = lines[0:6], other[0:6]
    extra[...] = jnp.zeros_like(extra)
    extra[0:6] = jnp.where(upper, given, mine)
    extra[6:12] = jnp.where(upper, mine, given)
    extra[12:13] = lines[6:7]
    extra[13:14] = beyond[6:7]
    far[SLAB * REACH :] = extra[0:16]
    near[SLAB * REACH :] = extra[0:16]


def pack(*args):
    shapes = (
        (SLAB * REACH + 16, LANES),
        (SLAB, ELEM, LANES),
        (SLAB * REACH + 16, LANES),
        (HALO, LANES),
    )
    vmem = pl.BlockSpec(memory_space=pltpu.VMEM)
    return pl.pallas_call(
        pack_body,
        out_shape=[jax.ShapeDtypeStruct(shape, F32) for shape in shapes],
        in_specs=[vmem] * len(args),
        out_specs=[vmem] * len(shapes),
        cost_estimate=pl.CostEstimate(flops=0, bytes_accessed=2000000, transcendentals=0),
        name="pack",
        compiler_params=pltpu.CompilerParams(vmem_limit_bytes=4 * 2**20),
    )(*args)


def near_base(odd):
    return 4 * (1 - odd)


def far_base(odd):
    return 6 * odd


def corner_body(tiles, is_far, own, one, two, three, part, *refs):
    if is_far:
        near, extra, chunk, motion, source, shifted, table = refs
    else:
        extra, chunk, near_target, source, shifted, table = refs
    tile = lax.axis_index("tile")
    depth = lax.axis_index("depth")
    odd = lax.rem(tile, 2)
    if is_far:
        motion[...] = jnp.zeros_like(motion)
        motion[1:2] = extra[12:13]
        motion[3:4] = extra[13:14]
        motion[pl.ds(2 * odd, 1)] = part[SLAB * REACH + 12 : SLAB * REACH + 13]
        motion[pl.ds(2 - 2 * odd, 1)] = near[SLAB * REACH + 12 : SLAB * REACH + 13]
    right = odd if is_far else 1 - odd
    base = far_base(odd) if is_far else near_base(odd)
    rows = pl.ds(8 + HALO - REACH + (ROWS + REACH) * right, REACH)
    for z in range(SLAB):
        source[z, rows] = part[z * REACH : (z + 1) * REACH]
    for step, piece in enumerate((own, one, two, three)):
        start = lax.rem(depth + step, 4) * 8
        source[pl.ds(start, 8), 8 + HALO : 8 + HALO + ROWS] = piece[0:8]
        if not is_far:
            edge = pl.ds(pl.multiple_of(ELEM * (1 - odd), 8), ELEM)
            near_target[pl.ds(start, 8)] = piece[8:16, edge]
    for e in range(2):
        for c in range(3):
            for which in range(2):
                at = e * 6 + c * 2 + which
                row = (e * 6 + which) * 3 + c
                table[row + 6 : row + 7] = extra[at : at + 1]
                line = part[SLAB * REACH + at : SLAB * REACH + at + 1]
                table[pl.ds(row + 12 * right, 1)] = line

    shape = (8, LANES)
    lanes = lane_ids(shape)
    zeros = jnp.zeros(shape, F32)

    def group(number, carry):
        v = base + number
        ex = (v + 1) // 2
        outside = ((tile == 0) & (v < 3)) | ((tile == tiles - 1) & (v >= 7))
        inside = jnp.where(outside, 0.0, 1.0).astype(F32)
        for e in range(2):
            offs = [
                jnp.broadcast_to(table[pl.ds((e * 6 + ex) * 3 + c, 1)], shape) for c in range(3)
            ]
            reach = lanes + offs[2].astype(jnp.int32)
            picks = []
            for s in range(2):
                at = reach + s
                good = jnp.where((at >= 0) & (at < LANES), inside, 0.0)
                picks.append((jnp.clip(at, 0, LANES - 1), good))
            is_x = [offs[1] == float(o) for o in (-2, -1, 0)]
            odd_z = (offs[0] == -1.0) | (offs[0] == 1.0)
            high_z = offs[0] >= 0.0
            planes = []
            steps = []
            for p in range(20):
                z = 16 * e + p - 2
                corners = [zeros] * 4
                if 0 <= z < SLAB:
                    for half in range(2):
                        block = source[z, pl.ds(8 * v + 6 + 4 * half, 8)]
                        for s in range(2):
                            index, good = picks[s]
                            taken = jnp.take_along_axis(
                                block, index, axis=1, mode="promise_in_bounds"
                            )
                            shifted[e, s, p, 4 * half : 4 * half + 8] = taken * good
                    corners = []
                    for sx in range(2):
                        for sy in range(2):
                            rows = [shifted[e, sy, p, sx + o : sx + o + 8] for o in range(4)]
                            corners.append(
                                jnp.where(
                                    is_x[0],
                                    rows[0],
                                    jnp.where(
                                        is_x[1], rows[1], jnp.where(is_x[2], rows[2], rows[3])
                                    ),
                                )
                            )
                planes.append(corners)
                if p >= 1:
                    steps.append(
                        [jnp.where(odd_z, planes[p][n], planes[p - 1][n]) for n in range(4)]
                    )
                if p >= 3:
                    c00, c01, c10, c11 = [
                        jnp.where(high_z, steps[p - 1][n], steps[p - 3][n]) for n in range(4)
                    ]
                    along = c01 - c00
                    chunk[number, e, p - 3, 0] = c00
                    chunk[number, e, p - 3, 1] = along
                    chunk[number, e, p - 3, 2] = c10 - c00
                    chunk[number, e, p - 3, 3] = (c11 - c10) - along
        return carry

    lax.fori_loop(0, chunk.shape[0], group, 0)


def corner_images(tiles, is_far, *args):
    vmem = pl.BlockSpec(memory_space=pltpu.VMEM)
    shapes = [(4 if is_far else 6, 2, 17, 4, 8, LANES)]
    shapes.append((8, LANES) if is_far else (SLAB, ELEM, LANES))
    return pl.pallas_call(
        functools.partial(corner_body, tiles, is_far),
        out_shape=[jax.ShapeDtypeStruct(shape, F32) for shape in shapes],
        in_specs=[vmem] * len(args),
        out_specs=[vmem] * len(shapes),
        scratch_shapes=[
            pltpu.VMEM((SLAB, FRAME + 16, LANES), F32),
            pltpu.VMEM((2, 2, 20, 16, LANES), F32),
            pltpu.VMEM((40, LANES), F32),
        ],
        cost_estimate=pl.CostEstimate(flops=5000000, bytes_accessed=4000000, transcendentals=0),
        name="corners_far" if is_far else "corners_near",
        compiler_params=pltpu.CompilerParams(vmem_limit_bytes=8 * 2**20),
    )(*args)


def updated_motion(motion, received, tile, tiles, padded):
    padded[...] = jnp.zeros_like(padded)
    padded[8 : 8 + tiles] = received[...]
    total = jnp.sum(received[...], axis=0, keepdims=True)
    descent = total[:, 96:97]
    length = total[:, 97:98]
    curvature = total[:, 98:99]
    step = descent / (curvature + LEVENBERG * length)
    near = padded[pl.ds(7 + tile, 8)]
    return motion[...] - step * near


def own_lanes():
    shape = (16, LANES)
    return (lane_ids(shape) // 8 == row_ids(shape)) & (row_ids(shape) < 12)


def warp_image(now, odd, near_cors, far_cors, along_y, wide, ends, warped):
    shape16 = (16, LANES)
    pick = own_lanes()
    spread = jnp.concatenate(
        [jnp.where(pick, jnp.broadcast_to(now[n : n + 1], shape16), 0.0) for n in range(4)], axis=0
    )
    wide[...] = exact_dot(spread, [along_y[...]])

    zero = jnp.zeros((2, FRAME, LANES), F32)
    warped[0:2] = zero
    warped[SLAB + 2 : SLAB + 4] = zero

    shares = (row_ids((8, LANES)).astype(F32) + 0.5) * (1.0 / ELEM)
    for v in range(GROUPS):
        node = (v + 1) // 2
        lower = 16 * (node // 2) + 6 * (node % 2)
        upper = 16 * ((node + 1) // 2) + 6 * ((node + 1) % 2)
        share = shares + 0.5 * ((v + 1) % 2)
        for n in range(6):
            begin = wide[lower + n : lower + n + 1]
            ends[v, n] = begin + share * (wide[upper + n : upper + n + 1] - begin)

    def warp(cors, base, number, carry):
        v = base + number
        at = pl.ds(pl.multiple_of(8 * v, 8), 8)
        near = [ends[v, 2 * c] for c in range(3)]
        far = [ends[v, 2 * c + 1] for c in range(3)]
        for e in range(2):
            if e == 0:
                move = [n + (f - n) * (1.0 / 32) for n, f in zip(near, far)]
                gain = [(f - n) * (1.0 / 16) for n, f in zip(near, far)]
            else:
                move = [f * (31.0 / 32) for f in far]
                gain = [f * (-1.0 / 16) for f in far]
            plane = [cors[number, e, 0, n] for n in range(4)]
            for j in range(16):
                above = [cors[number, e, j + 1, n] for n in range(4)]
                mz, mx, my = move
                here = (plane[0] + my * plane[1]) + mx * (plane[2] + my * plane[3])
                there = (above[0] + my * above[1]) + mx * (above[2] + my * above[3])
                warped[2 + 16 * e + j, at] = here + mz * (there - here)
                plane = above
                if j < 15:
                    move = [m + g for m, g in zip(move, gain)]
        return carry

    lax.fori_loop(0, 6, functools.partial(warp, near_cors, near_base(odd)), 0)
    lax.fori_loop(0, 4, functools.partial(warp, far_cors, far_base(odd)), 0)


def warp_body(motion, near_cors, far_cors, along_y, warped, wide, ends):
    odd = lax.rem(lax.axis_index("tile"), 2)
    warp_image(motion[...], odd, near_cors, far_cors, along_y, wide, ends, warped)


def first_warp(motion, cors, along_y):
    vmem = pl.BlockSpec(memory_space=pltpu.VMEM)
    return pl.pallas_call(
        warp_body,
        out_shape=jax.ShapeDtypeStruct((SLAB + 4, FRAME, LANES), F32),
        in_specs=[vmem] * 4,
        out_specs=vmem,
        scratch_shapes=[
            pltpu.VMEM((64, LANES), F32),
            pltpu.VMEM((GROUPS, 6, 8, LANES), F32),
        ],
        cost_estimate=pl.CostEstimate(flops=4000000, bytes_accessed=7000000, transcendentals=0),
        name="warp",
        compiler_params=pltpu.CompilerParams(vmem_limit_bytes=4 * 2**20),
    )(motion, *cors, along_y)


def iteration_body(tiles, first, last, *refs):
    refs = list(refs)
    motion = refs.pop(0)
    received = None if first else refs.pop(0)
    if first:
        pieces, refs = refs[:6], refs[6:]
    else:
        target = refs.pop(0)
    if first:
        warped = refs.pop(0)
    else:
        near_cors, far_cors, refs = refs[0], refs[1], refs[2:]
    along_y, over_y, over_y2, block_out, motion_out = refs[:5]
    refs = refs[5:]
    if first:
        target = refs.pop(0)
    residual_out = refs.pop(0) if last else None
    slopes, layers, rows_f, rows_s, padded = refs[:5]
    if not first:
        wide, ends, warped = refs[5:8]
    residuals = refs[8] if last else None

    tile = lax.axis_index("tile")
    odd = lax.rem(tile, 2)
    if first:
        depth = lax.axis_index("depth")
        for step, piece in enumerate(pieces[:4]):
            start = lax.rem(depth + step, 4) * 8
            target[pl.ds(start, 8), ELEM : ELEM + ROWS] = piece[8:16]
        far = pl.ds(pl.multiple_of((ELEM + ROWS) * odd, 8), ELEM)
        near = pl.ds(pl.multiple_of((ELEM + ROWS) * (1 - odd), 8), ELEM)
        target[:, far] = pieces[4][...]
        target[:, near] = pieces[5][...]
    low_flag = jnp.where(tile > 0, 1.0, 0.0).astype(F32)
    high_flag = jnp.where(tile < tiles - 1, 1.0, 0.0).astype(F32)
    now = motion[...] if first else updated_motion(motion, received, tile, tiles, padded)
    motion_out[...] = now
    if not first:
        warp_image(now, odd, near_cors, far_cors, along_y, wide, ends, warped)

    shape = (8, LANES)
    lanes = lane_ids(shape)
    ahead_1 = jnp.where(lanes < LANES - 1, 8.0, 0.0)
    behind_1 = jnp.where(lanes > 0, 8.0, 0.0)
    ahead_2 = jnp.where(lanes < LANES - 2, 1.0, 0.0)
    behind_2 = jnp.where(lanes > 1, 1.0, 0.0)
    zeros = jnp.zeros(shape, F32)

    def slope_group(v, own, misfit):
        at = pl.ds(aligned(8 * v), 8)
        row = aligned(8 * (v - 3))
        goal = pl.ds(aligned(8 * (v - 1)), 8)
        planes = [warped[n, at] for n in range(4)]
        for e in range(2):
            first_sum = [zeros] * 3
            second_sum = [zeros] * 3
            squares_0 = [zeros] * 3
            squares_1 = [zeros] * 3
            squares_2 = [zeros] * 3
            for j in range(16):
                z = 16 * e + j
                planes.append(warped[z + 4, at])
                mid = planes[2]
                slope_z = 8.0 * (planes[3] - planes[1]) - (planes[4] - planes[0])
                planes = planes[1:]
                up_1 = warped[z + 2, pl.ds(8 * v + 1, 8)]
                up_2 = warped[z + 2, pl.ds(8 * v + 2, 8)]
                down_1 = warped[z + 2, pl.ds(8 * v - 1, 8)]
                down_2 = warped[z + 2, pl.ds(8 * v - 2, 8)]
                slope_x = 8.0 * (up_1 - down_1) - (up_2 - down_2)
                slope_y = (
                    ahead_1 * pltpu.roll(mid, LANES - 1, 1) - behind_1 * pltpu.roll(mid, 1, 1)
                ) - (ahead_2 * pltpu.roll(mid, LANES - 2, 1) - behind_2 * pltpu.roll(mid, 2, 1))
                residual = mid - target[z, goal]
                three = (slope_z, slope_x, slope_y)
                if own:
                    misfit = misfit + residual * residual
                    for c in range(3):
                        slopes[c, z, pl.ds(row, 8)] = three[c]
                    if last:
                        residuals[z, pl.ds(row, 8)] = residual
                weight = 1.0 - (j + 0.5) / 16.0
                for c in range(3):
                    first_sum[c] = first_sum[c] + three[c] * residual
                    second_sum[c] = second_sum[c] + first_sum[c]
                    square = three[c] * three[c]
                    if e == 0:
                        squares_0[c] = squares_0[c] + square
                        squares_1[c] = squares_1[c] + squares_0[c]
                        squares_2[c] = squares_2[c] + squares_1[c]
                    else:
                        squares_0[c] = squares_0[c] + (weight * weight) * square
            for c in range(3):
                falling = (second_sum[c] - 0.5 * first_sum[c]) * (1.0 / 16)
                if e == 0:
                    layers[v - 1, 2 * c] = falling
                    layers[v - 1, 2 * c + 1] = first_sum[c] - falling
                    line = (squares_1[c] - 0.5 * squares_0[c]) * (1.0 / 16)
                    both = (squares_2[c] - squares_1[c]) * (1.0 / 128) + squares_0[c] * (1.0 / 1024)
                    layers[v - 1, 6 + 2 * c] = both
                    layers[v - 1, 6 + 2 * c + 1] = (squares_0[c] - 2.0 * line) + both
                else:
                    layers[v - 1, 2 * c + 1] += falling
                    layers[v - 1, 6 + 2 * c + 1] += squares_0[c]
        return misfit

    def two_groups(number, misfit):
        misfit = slope_group(3 + 2 * number, True, misfit)
        return slope_group(4 + 2 * number, True, misfit)

    slope_group(1, False, zeros)
    slope_group(2, False, zeros)
    misfit = lax.fori_loop(0, 2, two_groups, zeros)
    slope_group(7, False, zeros)
    slope_group(8, False, zeros)

    if last:
        leaving = pltpu.make_async_copy(
            residuals.at[pl.ds(lax.axis_index("depth") * 8, 8)], residual_out, refs[9].at[0]
        )
        leaving.start()
    rows_f[...] = jnp.zeros_like(rows_f)
    rows_s[...] = jnp.zeros_like(rows_s)
    rows8 = row_ids((8, 1)).astype(F32)
    for k in range(3):
        sums = [zeros] * 12
        for v in range(1 + 2 * k, 5 + 2 * k):
            weight = 1.0 - jnp.abs((8 * v - HALO - ELEM * k) + 0.5 + rows8) * (1.0 / ELEM)
            square = weight * weight
            if v < 3:
                weight, square = weight * low_flag, square * low_flag
            if v >= 7:
                weight, square = weight * high_flag, square * high_flag
            for n in range(12):
                sums[n] = sums[n] + (weight if n < 6 else square) * layers[v - 1, n]
        for n in range(6):
            at = k * 6 + n
            rows_f[at : at + 1] = jnp.sum(sums[n], axis=0, keepdims=True)
            rows_s[at : at + 1] = jnp.sum(sums[6 + n], axis=0, keepdims=True)
    force = exact_dot(rows_f[...], [over_y[...]]) * (1.0 / 12)
    stiffness = exact_dot(rows_s[...], [over_y2[0], over_y2[1]]) * (1.0 / 144)
    shape24 = (24, LANES)
    rows24 = row_ids(shape24)
    lanes24 = lane_ids(shape24)
    direction = force / (stiffness + LEVENBERG)
    direction = jnp.where(rows24 < 12, direction, direction * high_flag)
    held = jnp.where(lanes24 < 8, direction, 0.0)
    owned = jnp.where(rows24 < 12, held, 0.0)
    descent = jnp.sum(force * owned)
    length = jnp.sum(owned * owned)
    rows_f[...] = exact_dot(held, [along_y[...]])
    curved = zeros
    for v in range(3, 7):
        k = (v - 3) // 2
        share = (8.0 * ((v - 3) % 2) + 0.5 + rows8) * (1.0 / ELEM)
        field = []
        for n in range(6):
            near = rows_f[k * 6 + n : k * 6 + n + 1]
            far = rows_f[k * 6 + 6 + n : k * 6 + 7 + n]
            field.append(near + share * (far - near))
        row = 8 * (v - 3)
        for e in range(2):
            if e == 0:
                move = [field[2 * c] + (field[2 * c + 1] - field[2 * c]) * (1.0 / 32) for c in range(3)]
                gain = [(field[2 * c + 1] - field[2 * c]) * (1.0 / 16) for c in range(3)]
            else:
                move = [field[2 * c + 1] for c in range(3)]
            for j in range(16):
                three = [slopes[c, 16 * e + j, row : row + 8] for c in range(3)]
                projected = (three[0] * move[0] + three[1] * move[1]) + three[2] * move[2]
                projected = projected * projected
                if e == 1:
                    projected = projected * (1.0 - (j + 0.5) / 16.0) ** 2
                curved = curved + projected
                if e == 0 and j < 15:
                    move = [m + g for m, g in zip(move, gain)]
    curvature = jnp.sum(curved) * (1.0 / 144)
    misfit = jnp.sum(misfit)
    line = jnp.sum(jnp.where(own_lanes(), direction[0:16], 0.0), axis=0, keepdims=True)
    line_lanes = lane_ids((1, LANES))
    for at, value in ((96, descent), (97, length), (98, curvature), (99, misfit)):
        line = jnp.where(line_lanes == at, value, line)
    block_out[...] = jnp.broadcast_to(line, (tiles, LANES))
    if last:
        leaving.wait()


def iteration(tiles, first, last, motion, received, target, cors, tables):
    vmem = pl.BlockSpec(memory_space=pltpu.VMEM)
    args = [motion] + ([] if first else [received]) + [*target, *cors, *tables]
    shapes = [
        jax.ShapeDtypeStruct((tiles, LANES), F32),
        jax.ShapeDtypeStruct((8, LANES), F32),
    ]
    scratch = [
        pltpu.VMEM((3, SLAB, ROWS, LANES), F32),
        pltpu.VMEM((8, 12, 8, LANES), F32),
        pltpu.VMEM((24, LANES), F32),
        pltpu.VMEM((24, LANES), F32),
        pltpu.VMEM((tiles + 24, LANES), F32),
    ]
    if not first:
        scratch += [
            pltpu.VMEM((64, LANES), F32),
            pltpu.VMEM((GROUPS, 6, 8, LANES), F32),
            pltpu.VMEM((SLAB + 4, FRAME, LANES), F32),
        ]
    if first:
        shapes.append(jax.ShapeDtypeStruct((SLAB, ROWS + 2 * ELEM, LANES), F32))
    if last:
        shapes.append(jax.ShapeDtypeStruct((8, ROWS, LANES), F32))
        scratch.append(pltpu.VMEM((SLAB, ROWS, LANES), F32))
        scratch.append(pltpu.SemaphoreType.DMA((1,)))
    out_specs = [vmem] * len(shapes)
    if last:
        out_specs[-1] = pl.BlockSpec(memory_space=pltpu.HBM)
    return pl.pallas_call(
        functools.partial(iteration_body, tiles, first, last),
        out_shape=shapes,
        in_specs=[vmem] * len(args),
        out_specs=out_specs,
        scratch_shapes=scratch,
        cost_estimate=pl.CostEstimate(flops=20000000, bytes_accessed=9000000, transcendentals=0),
        name="iteration",
        compiler_params=pltpu.CompilerParams(vmem_limit_bytes=16 * 2**20),
    )(*args)


def finish_body(tiles, motion, got_1, got_2, got_3, chooser, displacement, misfits, padded):
    now = updated_motion(motion, got_3, lax.axis_index("tile"), tiles, padded)
    shape = (8, LANES)
    component = (lane_ids(shape) // 16) % 3
    mine = jnp.where(component == row_ids(shape), jnp.broadcast_to(now[1:2], shape), 0.0)
    mine = jnp.where(lane_ids(shape) < 96, mine, 0.0)
    placed = exact_dot(mine, [chooser[...]])
    displacement[...] = placed[0:3, 0:32]
    for n, got in enumerate((got_1, got_2, got_3)):
        total = jnp.sum(got[...], axis=0, keepdims=True)
        misfits[:, n : n + 1] = total[:, 99:100] * (1.0 / VOXELS)


def finish(tiles, motion, got, chooser):
    vmem = pl.BlockSpec(memory_space=pltpu.VMEM)
    return pl.pallas_call(
        functools.partial(finish_body, tiles),
        out_shape=[jax.ShapeDtypeStruct((3, 32), F32), jax.ShapeDtypeStruct((1, 3), F32)],
        in_specs=[vmem] * 5,
        out_specs=[vmem] * 2,
        scratch_shapes=[pltpu.VMEM((tiles + 24, LANES), F32)],
        name="finish",
        compiler_params=pltpu.CompilerParams(vmem_limit_bytes=2**20),
    )(motion, *got, chooser)


def from_behind(block, axis, distance):
    devices = range(lax.axis_size(axis))
    return lax.ppermute(block, axis, [(i - distance, i) for i in devices if i - distance in devices])


def swap(block, first):
    pairs = [(i, i + 1) for i in range(first, lax.axis_size("tile") - 1, 2)]
    return lax.ppermute(block, "tile", pairs + [(j, i) for i, j in pairs])


def ring(block, distance):
    peers = lax.axis_size("depth")
    return lax.ppermute(block, "depth", [((i + distance) % peers, i) for i in range(peers)])


def local(reference_image, deformed_image, offsets, node_ids, start_motion):
    tiles = lax.axis_size("tile")
    zero = jnp.zeros((), F32)
    both = lax.pad(deformed_image, zero, ((0, 8, 0), (0, 0, 0), (0, 0, 0)))
    both = both + lax.pad(reference_image, zero, ((8, 0, 0), (0, 0, 0), (0, 0, 0)))
    both = [both] + [ring(both, n) for n in (1, 2, 3)]
    lines, chooser, *tables = prepare(offsets, node_ids, start_motion)
    other = ring(lines, 2)
    beyond = from_behind(lines, "tile", -2)
    far, far_target, near, extra = pack(*both, lines, other, beyond)
    far = swap(far, 1)
    near = swap(near, 0)
    far_target = swap(far_target, 1)
    near_cors, near_target = corner_images(tiles, False, *both, near, extra)
    near_target = swap(near_target, 0)
    far_cors, motion = corner_images(tiles, True, *both, far, near, extra)
    cors = (near_cors, far_cors)
    warped = first_warp(motion, cors, tables[0])
    target = (*both, far_target, near_target)
    received = None
    got = []
    for number in range(ITERS):
        first, last = number == 0, number == ITERS - 1
        sources = (warped,) if first else cors
        outs = iteration(tiles, first, last, motion, received, target, sources, tables)
        block, motion = outs[:2]
        if first:
            target = (outs[2],)
        received = lax.all_to_all(block, "tile", 0, 0, tiled=True)
        got.append(received)
    displacement, misfits = finish(tiles, motion, got, chooser)
    return displacement, misfits.reshape(3), outs[2]


def solution(mesh):
    in_specs = (
        P("depth", "tile", None),
        P("depth", "tile", None),
        P(None, "depth", "tile", None),
        P(None, "tile", None),
        P(None, "tile"),
    )
    out_specs = (P(None, "tile"), P(), P("depth", "tile", None))
    return jax.shard_map(local, mesh=mesh, in_specs=in_specs, out_specs=out_specs, check_vma=False)
```
